256 devices in a mesh: blk: 16 (over z_lo, y, core), ulysses: 16 (over z_hi, x).
Axes of the slice: x: 4, y: 4, z: 8 (z_hi: 4, z_lo: 2; z = z_hi * 2 + z_lo), core: 2. Of those that a mesh axis runs over, the one named last changes fastest.
Arguments:
- query_tokens: bfloat16 [32768, 4096], P(('blk', 'ulysses')), may hold values from -5 to 5
- key_tokens: bfloat16 [32768, 4096], P(('blk', 'ulysses')), may hold values from -5 to 5
- value_tokens: bfloat16 [32768, 4096], P(('blk', 'ulysses')), may hold values from -5 to 5
- cotangent: bfloat16 [32768, 4096], P(('blk', 'ulysses')), may hold values from -5 to 5
- block_mask: int32 [256, 256], replicated, may hold values from 0 to 1, as said below
Outputs:
- attended: bfloat16 [32768, 4096], P(('blk', 'ulysses'))
- grad_query: bfloat16 [32768, 4096], P(('blk', 'ulysses'))
- grad_key: bfloat16 [32768, 4096], P(('blk', 'ulysses'))
- grad_value: bfloat16 [32768, 4096], P(('blk', 'ulysses'))
The draws below stay inside these ranges and needn't reach their ends.
Inputs may be any that keep to these rules, and one draw needn't show every extreme that they name: block_mask is symmetric. A span is a run of 16 consecutive blocks. Inside a span, block s attends block s2 exactly when they differ by at most one. A query block attends at most one key block in each other span. The queries of one span attend keys of exactly 7 other spans, and at most 2 distinct key blocks of any other span; in every draw some pairs of spans reach 2.
All inputs are finite; a program needn't handle non-finite values.
Results may differ from the reference program's by a relative error of at most 0.0096.
Values may be sent and summed in bfloat16 or wider, within the bound.
A program may use at most 128 MiB of HBM per device.

```python
import math
import jax
import jax.numpy as jnp
from jax import lax

HEADS = 32
HEAD_DIM = 128
BLOCK = 128
TOKENS = 32768
NBLOCKS = 256
SPAN_BLOCKS = 16
LINKS = 7
N_BLK = 16


def draw_query_tokens(key, part):
    shape = (TOKENS, HEADS * HEAD_DIM)
    row_scale = jnp.exp(jax.random.uniform(jax.random.fold_in(key, 3), (TOKENS, 1), minval=math.log(0.15), maxval=math.log(1.5)))
    noise = jax.random.truncated_normal(jax.random.fold_in(key, 1), -3.0, 3.0, shape)
    result = noise * row_scale
    return result.astype(jnp.bfloat16)


def draw_key_tokens(key, part):
    shape = (TOKENS, HEADS * HEAD_DIM)
    result = jax.random.truncated_normal(jax.random.fold_in(key, 2), -4.0, 4.0, shape)
    return result.astype(jnp.bfloat16)


def draw_block_mask(key, part):
    log_span = SPAN_BLOCKS.bit_length() - 1
    link_count = LINKS
    subkeys = jax.random.split(jax.random.fold_in(key, 11), 5)
    partner_high = jax.random.permutation(subkeys[0], N_BLK - 1)[:link_count].astype(jnp.int32) + 1
    free_bit = jax.random.randint(subkeys[1], (link_count,), 0, log_span)
    use_bit = jax.random.randint(subkeys[2], (link_count,), 0, 2)
    narrow = jax.random.randint(subkeys[3], (link_count,), 0, 2).at[0].set(0)
    bit_value = jnp.left_shift(jnp.ones((link_count,), jnp.int32), free_bit)
    all_bits = SPAN_BLOCKS - 1
    keep_bits = jnp.where(narrow == 1, all_bits, all_bits - bit_value)
    flip_bits = jnp.where(narrow == 1, 0, use_bit * bit_value)
    offsets = jax.random.randint(subkeys[4], (link_count, N_BLK), 0, SPAN_BLOCKS)
    blocks = jnp.arange(NBLOCKS, dtype=jnp.int32)
    span_of = blocks // SPAN_BLOCKS
    spot_of = blocks % SPAN_BLOCKS
    row_span = span_of[:, None]
    col_span = span_of[None, :]
    row_spot = spot_of[:, None]
    col_spot = spot_of[None, :]
    banded = (row_span == col_span) & (jnp.abs(row_spot - col_spot) <= 1)
    linked = banded
    for index_k in range(link_count):
        pair_id = jnp.minimum(span_of, span_of ^ partner_high[index_k])
        target = offsets[index_k][pair_id] & keep_bits[index_k]
        row_holds = spot_of & keep_bits[index_k] == target
        linked_now = (col_span == row_span ^ partner_high[index_k]) & (col_spot == row_spot ^ flip_bits[index_k]) & row_holds[:, None]
        linked = linked | linked_now
    return linked.astype(jnp.int32)


def levels(rng, dims, pieces, least, top_value):
    level, own = 1.0, jax.random.fold_in(rng, 6)
    for axis_at, blocks in pieces:
        draws = jnp.exp(jax.random.uniform(jax.random.fold_in(own, axis_at), (blocks,), jnp.float32, least / len(pieces), top_value / len(pieces)))
        level = level * jnp.repeat(draws, dims[axis_at] // blocks).reshape([-1 if axis == axis_at else 1 for axis in range(len(dims))])
    return level


def bell_draw(stream_key, dims, scale, reach, pieces=(), held_as=jnp.bfloat16):
    drawn = scale * jax.random.normal(stream_key, dims, jnp.float32)
    if pieces:
        drawn = drawn * levels(stream_key, dims, pieces, -0.22, 0.18)
    return jnp.clip(drawn, -reach, reach).astype(held_as)


def setup_inputs(seed: int = 0) -> dict:
    seeds = jax.random.split(jax.random.key(seed), 6)
    return {
        "query_tokens": draw_query_tokens(jax.random.fold_in(seeds[5], 71), 0),
        "key_tokens": draw_key_tokens(jax.random.fold_in(seeds[5], 71), 0),
        "value_tokens": bell_draw(seeds[2], (TOKENS, HEADS * HEAD_DIM), 1.0, 5.0, ((0, 256),)),
        "cotangent": bell_draw(seeds[3], (TOKENS, HEADS * HEAD_DIM), 1.0, 5.0, ((0, 256),)),
        "block_mask": draw_block_mask(jax.random.fold_in(seeds[5], 71), 0),
    }


def round_trip(tensor):
    return lax.optimization_barrier(tensor.astype(jnp.bfloat16)).astype(jnp.float32)


def head_pass(blocks, index_list, is_valid):
    queries, keyset, values, upstream = blocks
    score_scale = HEAD_DIM ** -0.5
    query_f = queries.astype(jnp.float32)
    upstream_f = upstream.astype(jnp.float32)
    key_tiles = keyset[index_list].astype(jnp.float32)
    value_tiles = values[index_list].astype(jnp.float32)
    scores = jnp.einsum('ird,itcd->itrc', query_f, key_tiles) * score_scale
    scores = jnp.where(is_valid[:, :, None, None], scores, -jnp.inf)
    row_peak = jnp.max(scores, axis=(1, 3))
    row_total = jnp.sum(jnp.exp(scores - row_peak[:, None, :, None]), axis=(1, 3))
    log_total = row_peak + jnp.log(row_total)
    probability = jnp.exp(scores - log_total[:, None, :, None])
    weights = round_trip(probability)
    output = jnp.einsum('itrc,itcd->ird', weights, value_tiles)
    row_delta = jnp.sum(upstream_f * output, axis=2)
    grad_prob = jnp.einsum('ird,itcd->itrc', upstream_f, value_tiles)
    dscore = round_trip(probability * (grad_prob - row_delta[:, None, :, None]))
    grad_q = jnp.einsum('itrc,itcd->ird', dscore, key_tiles) * score_scale
    key_terms = jnp.einsum('itrc,ird->itcd', dscore, query_f) * score_scale
    value_terms = jnp.einsum('itrc,ird->itcd', weights, upstream_f)
    grad_k = jnp.zeros_like(query_f).at[index_list].add(key_terms)
    grad_v = jnp.zeros_like(query_f).at[index_list].add(value_terms)
    return (output.astype(jnp.bfloat16), grad_q.astype(jnp.bfloat16),
            grad_k.astype(jnp.bfloat16), grad_v.astype(jnp.bfloat16))


def split_heads(tensor):
    return tensor.reshape(NBLOCKS, BLOCK, HEADS, HEAD_DIM).transpose(2, 0, 1, 3)


def merge_heads(tensor):
    return tensor.transpose(1, 2, 0, 3).reshape(TOKENS, HEADS * HEAD_DIM)


def reference(query_tokens, key_tokens, value_tokens, cotangent, block_mask):
    list_width = 3 + LINKS
    block_count = NBLOCKS
    ranking = block_mask * block_count + (block_count - 1 - lax.broadcasted_iota(jnp.int32, (block_count, block_count), 1))
    ranked, index_list = lax.top_k(ranking, list_width)
    index_list = index_list.astype(jnp.int32)
    is_valid = ranked >= block_count

    def one_head(blocks):
        return head_pass(blocks, index_list, is_valid)

    stacked = (split_heads(query_tokens), split_heads(key_tokens), split_heads(value_tokens), split_heads(cotangent))
    results = lax.map(one_head, stacked)
    return (merge_heads(results[0]), merge_heads(results[1]), merge_heads(results[2]), merge_heads(results[3]))
```

```python
import functools

import jax
import jax.numpy as jnp
from jax import lax
from jax.experimental import pallas as pl
from jax.experimental.pallas import tpu as pltpu
from jax.sharding import PartitionSpec as P

HEAD_DIM = 128
BLOCK = 128
NEED = 2
LINKS = 7
MESH = pl.DeviceIdType.MESH
BF16 = jnp.bfloat16
F32 = jnp.float32
ANY = pl.BlockSpec(memory_space=pl.ANY)
VMEM = pl.BlockSpec(memory_space=pltpu.VMEM)
SMEM = pl.BlockSpec(memory_space=pltpu.SMEM)


def greet(groups, members):
    b, u = lax.axis_index("blk"), lax.axis_index("ulysses")
    barrier = pltpu.get_barrier_semaphore()
    for t in range(1, members):
        pl.semaphore_signal(
            barrier, inc=1, device_id=(b, lax.rem(u + t, members)), device_id_type=MESH
        )
    for t in range(1, groups):
        pl.semaphore_signal(
            barrier, inc=1, device_id=(lax.rem(b + t, groups), u), device_id_type=MESH
        )
    pl.semaphore_wait(barrier, members + groups - 2)


def wait_bytes(ref, sem):
    pltpu.make_async_copy(ref, ref, sem).wait()


def columns(index, width):
    return pl.ds(pl.multiple_of(index * width, width), width)


def gather_kernel(
    groups, members, pick, q, k, v, g, hq, hk, hv, hg, fk, fv,
    land_k, land_v, slots_k, slots_v, send, recv, own, blk_send, blk_recv,
):
    b, u = lax.axis_index("blk"), lax.axis_index("ulysses")
    width = land_k.shape[2]
    greet(groups, members)
    pairs = ((k, land_k), (v, land_v), (q, hq), (g, hg))

    def spread(n):
        src, dst = pairs[n]
        for t in range(1, members):
            to = lax.rem(u + t, members)
            pltpu.make_async_remote_copy(
                src_ref=src.at[:, columns(to, width)],
                dst_ref=dst.at[u],
                send_sem=send.at[n],
                recv_sem=recv.at[n],
                device_id=(b, to),
                device_id_type=MESH,
            ).start()
        pltpu.make_async_copy(src.at[:, columns(u, width)], dst.at[u], own.at[n]).start()

    def landed(n):
        dst = pairs[n][1]
        wait_bytes(dst.at[pl.ds(0, members - 1)], recv.at[n])
        wait_bytes(dst.at[0], own.at[n])

    spread(0)
    spread(1)
    landed(0)
    landed(1)
    keep_k = pltpu.make_async_copy(land_k, hk, own.at[4])
    keep_v = pltpu.make_async_copy(land_v, hv, own.at[5])
    keep_k.start()
    keep_v.start()
    spread(2)
    spread(3)
    for n, (land, slots, out) in enumerate(((land_k, slots_k, fk), (land_v, slots_v, fv))):
        for t in range(1, groups):
            to = lax.rem(b + t, groups)
            for s in range(NEED):
                slots[t, s] = land[pick[to, s]]
            pltpu.make_async_remote_copy(
                src_ref=slots.at[t],
                dst_ref=out.at[b],
                send_sem=blk_send.at[n],
                recv_sem=blk_recv.at[n],
                device_id=(to, u),
                device_id_type=MESH,
            ).start()
    landed(2)
    landed(3)
    keep_k.wait()
    keep_v.wait()
    for n, out in enumerate((fk, fv)):
        wait_bytes(out.at[pl.ds(0, groups - 1)], blk_recv.at[n])
        wait_bytes(out.at[pl.ds(0, groups - 1)], blk_send.at[n])
    for n in range(4):
        wait_bytes(hq.at[pl.ds(0, members - 1)], send.at[n])


def dot(a, b, contract):
    return lax.dot_general(a, b, ((contract[:1], contract[1:]), ((), ())), preferred_element_type=F32)


def attend_kernel(listed, count, q, k, v, g, fk, fv, o, dq, dk, dv, pk, pv, tiles):
    span = q.shape[0]
    heads = q.shape[2] // HEAD_DIM
    scale = HEAD_DIM ** (-0.5)
    dk[...] = jnp.zeros_like(dk)
    dv[...] = jnp.zeros_like(dv)

    @pl.loop(0, span)
    def _(i):
        start = jnp.clip(i - 1, 0, span - 3)
        n = count[i]
        column = lax.broadcasted_iota(jnp.int32, (BLOCK, 3 * BLOCK), 1) + start * BLOCK
        inside = (column >= (i - 1) * BLOCK) & (column < (i + 2) * BLOCK)
        for h in range(heads):
            hs = slice(h * HEAD_DIM, (h + 1) * HEAD_DIM)
            qi, gi = q[i, :, hs], g[i, :, hs]
            kw = k[pl.ds(start, 3), :, hs].reshape(3 * BLOCK, HEAD_DIM)
            vw = v[pl.ds(start, 3), :, hs].reshape(3 * BLOCK, HEAD_DIM)
            scores = jnp.where(inside, dot(qi, kw, (1, 1)) * scale, -jnp.inf)

            def score(e, peak):
                tile = dot(qi, fk[listed[i, e], :, hs], (1, 1)) * scale
                tiles[h, e] = tile
                return jnp.maximum(peak, jnp.max(tile, axis=1, keepdims=True))

            peak = lax.fori_loop(0, n, score, jnp.max(scores, axis=1, keepdims=True))
            raised = jnp.exp(scores - peak)

            def weigh(e, carry):
                total, out = carry
                tile = jnp.exp(tiles[h, e] - peak)
                tiles[h, e] = tile
                return total + jnp.sum(tile, axis=1, keepdims=True), out

            total, _ = lax.fori_loop(0, n, weigh, (jnp.sum(raised, axis=1, keepdims=True), 0))
            inverse = 1.0 / total
            prob = raised * inverse
            weights = prob.astype(BF16)

            def output(e, out):
                tile = tiles[h, e] * inverse
                tiles[h, e] = tile
                return out + dot(tile.astype(BF16), fv[listed[i, e], :, hs], (1, 0))

            out = lax.fori_loop(0, n, output, dot(weights, vw, (1, 0)))
            o[i, :, hs] = out.astype(BF16)
            delta = jnp.sum(gi.astype(F32) * out, axis=1, keepdims=True)
            dscore = (prob * (dot(gi, vw, (1, 1)) - delta)).astype(BF16)
            dk[pl.ds(start, 3), :, hs] += dot(dscore, qi, (0, 0)).reshape(3, BLOCK, HEAD_DIM)
            dv[pl.ds(start, 3), :, hs] += dot(weights, gi, (0, 0)).reshape(3, BLOCK, HEAD_DIM)

            def grads(e, total):
                slot = listed[i, e]
                tile = tiles[h, e]
                ds = (tile * (dot(gi, fv[slot, :, hs], (1, 1)) - delta)).astype(BF16)
                pk[slot, :, hs] = (dot(ds, qi, (0, 0)) * scale).astype(BF16)
                pv[slot, :, hs] = dot(tile.astype(BF16), gi, (0, 0)).astype(BF16)
                return total + dot(ds, fk[slot, :, hs], (1, 0))

            grad = lax.fori_loop(0, n, grads, dot(dscore, kw, (1, 0)))
            dq[i, :, hs] = (grad * scale).astype(BF16)


def scatter_kernel(
    groups, members, listed, o, dq, dk, dv, pk, pv, out_o, out_q, out_k, out_v,
    back_k, back_v, sum_k, sum_v, send, recv, own, blk_send, blk_recv,
):
    b, u = lax.axis_index("blk"), lax.axis_index("ulysses")
    width = o.shape[2]
    scale = HEAD_DIM ** (-0.5)
    greet(groups, members)
    for n, (part, back) in enumerate(((pk, back_k), (pv, back_v))):
        for t in range(1, groups):
            to = lax.rem(b + t, groups)
            pltpu.make_async_remote_copy(
                src_ref=part.at[to],
                dst_ref=back.at[pl.ds(pl.multiple_of(b * NEED, NEED), NEED)],
                send_sem=blk_send.at[n],
                recv_sem=blk_recv.at[n],
                device_id=(to, u),
                device_id_type=MESH,
            ).start()

    def start_one(n, src, dst, t):
        to = lax.rem(u + t, members)
        pltpu.make_async_remote_copy(
            src_ref=src.at[to],
            dst_ref=dst.at[:, columns(u, width)],
            send_sem=send.at[n],
            recv_sem=recv.at[n],
            device_id=(b, to),
            device_id_type=MESH,
        ).start()

    def start_own(n, src, dst):
        pltpu.make_async_copy(src.at[u], dst.at[:, columns(u, width)], own.at[n]).start()

    for n, (src, dst) in enumerate(((o, out_o), (dq, out_q))):
        for t in range(1, members):
            start_one(n, src, dst, t)
        start_own(n, src, dst)
    for n, (own_part, back, summed, dst, factor) in enumerate(
        ((dk, back_k, sum_k, out_k, scale), (dv, back_v, sum_v, out_v, 1.0))
    ):
        back[groups * NEED] = jnp.zeros(back.shape[1:], BF16)
        wait_bytes(back.at[pl.ds(0, (groups - 1) * NEED)], blk_recv.at[n])
        for t in range(members):
            j = lax.rem(u + 1 + t, members)
            total = own_part[j] * factor
            for e in range(LINKS):
                total = total + back[listed[j, e]].astype(F32)
            summed[j] = total.astype(BF16)
            if t < members - 1:
                start_one(2 + n, summed, dst, t + 1)
        start_own(2 + n, summed, dst)
    for n, dst in enumerate((out_o, out_q, out_k, out_v)):
        wait_bytes(dst.at[:, pl.ds(0, (members - 1) * width)], recv.at[n])
        wait_bytes(dst.at[:, pl.ds(0, (members - 1) * width)], send.at[n])
        wait_bytes(dst.at[:, pl.ds(0, width)], own.at[n])
    for n in range(2):
        wait_bytes(back_k.at[pl.ds(0, (groups - 1) * NEED)], blk_send.at[n])


def tables(block_mask, span, groups, group_id):
    rows = lax.dynamic_slice_in_dim(block_mask, group_id * span, span, 0)
    iota = lambda shape, axis: lax.broadcasted_iota(jnp.int32, shape, axis)
    cube = rows.reshape(span, groups, span) * (iota((span, groups, span), 1) != group_id)
    wanted = jnp.max(cube, axis=0)
    before = (iota((span, span), 0) < iota((span, span), 1)).astype(jnp.int32)
    rank_in = jnp.sum(wanted[:, :, None] * before[None], axis=1)
    has = jnp.sum(cube, axis=2)
    slot_in = jnp.sum(cube * rank_in[None], axis=2)
    before_c = (iota((groups, groups), 0) < iota((groups, groups), 1)).astype(jnp.int32)
    place = jnp.sum(has[:, :, None] * before_c[None], axis=1)
    rank_out = jnp.sum(has[:, None, :] * before[:, :, None], axis=0)
    partner = iota((span, groups), 1)
    spot = iota((span, groups), 0)
    chosen = has[:, :, None] * (place[:, :, None] == iota((span, groups, LINKS), 2))
    list_in = jnp.sum(chosen * (partner * NEED + slot_in)[:, :, None], axis=1)
    list_out = jnp.sum(chosen * (partner * NEED + rank_out)[:, :, None], axis=1)
    count = jnp.sum(has, axis=1)
    list_out = jnp.where(
        iota((span, LINKS), 1) < count[:, None], list_out, groups * NEED
    )
    pick = jnp.sum(
        (has * spot)[:, :, None] * (rank_out[:, :, None] == iota((span, groups, NEED), 2)), axis=0
    )
    return pick, list_in, count, list_out


def shards(query_tokens, key_tokens, value_tokens, cotangent, block_mask):
    groups, members = lax.axis_size("blk"), lax.axis_size("ulysses")
    group_id = lax.axis_index("blk")
    tokens, model = query_tokens.shape
    span = members * tokens // BLOCK
    width = model // members
    pick, list_in, count, list_out = tables(block_mask, span, groups, group_id)
    blocks = jax.ShapeDtypeStruct((span, BLOCK, width), BF16)
    slots = jax.ShapeDtypeStruct((groups, NEED, BLOCK, width), BF16)
    dma = pltpu.SemaphoreType.DMA
    params = functools.partial(pltpu.CompilerParams, vmem_limit_bytes=56 * 2**20)
    hq, hk, hv, hg, fk, fv = pl.pallas_call(
        functools.partial(gather_kernel, groups, members),
        out_shape=(blocks,) * 4 + (slots,) * 2,
        in_specs=[SMEM] + [ANY] * 4,
        out_specs=(ANY,) * 6,
        scratch_shapes=[
            pltpu.VMEM(blocks.shape, BF16),
            pltpu.VMEM(blocks.shape, BF16),
            pltpu.VMEM(slots.shape, BF16),
            pltpu.VMEM(slots.shape, BF16),
            dma((4,)),
            dma((4,)),
            dma((6,)),
            dma((2,)),
            dma((2,)),
        ],
        compiler_params=params(collective_id=0, has_side_effects=True),
        name="gather",
    )(pick, query_tokens, key_tokens, value_tokens, cotangent)
    flat = (groups * NEED, BLOCK, width)
    wide = jax.ShapeDtypeStruct(blocks.shape, F32)
    parts = jax.ShapeDtypeStruct(flat, BF16)
    o, dq, dk, dv, pk, pv = pl.pallas_call(
        attend_kernel,
        out_shape=(blocks, blocks, wide, wide, parts, parts),
        in_specs=[SMEM] * 2 + [VMEM] * 6,
        out_specs=(VMEM,) * 6,
        scratch_shapes=[pltpu.VMEM((width // HEAD_DIM, LINKS, BLOCK, BLOCK), F32)],
        compiler_params=params(),
        name="attend",
    )(list_in, count, hq, hk, hv, hg, fk.reshape(flat), fv.reshape(flat))
    back = pltpu.VMEM((groups * NEED + 1, BLOCK, width), BF16)
    whole = jax.ShapeDtypeStruct((tokens, model), BF16)
    return pl.pallas_call(
        functools.partial(scatter_kernel, groups, members),
        out_shape=(whole,) * 4,
        in_specs=[SMEM] + [ANY] * 2 + [VMEM] * 2 + [ANY] * 2,
        out_specs=(ANY,) * 4,
        scratch_shapes=[
            back,
            back,
            pltpu.VMEM(blocks.shape, BF16),
            pltpu.VMEM(blocks.shape, BF16),
            dma((4,)),
            dma((4,)),
            dma((4,)),
            dma((2,)),
            dma((2,)),
        ],
        compiler_params=params(collective_id=1, has_side_effects=True),
        name="scatter",
    )(list_out, o, dq, dk, dv, pk.reshape(slots.shape), pv.reshape(slots.shape))


def solution(mesh):
    placed = P(("blk", "ulysses"), None)
    return jax.shard_map(
        shards,
        mesh=mesh,
        in_specs=(placed,) * 4 + (P(),),
        out_specs=(placed,) * 4,
        check_vma=False,
    )
```

```python
import functools
import math

import jax
import jax.numpy as jnp
from jax import lax
from jax.experimental import pallas as pl
from jax.experimental.pallas import tpu as pltpu
from jax.sharding import PartitionSpec as P

HEAD_DIM = 128
BLOCK = 128
NEED = 2
LINKS = 7
EDGES = NEED * LINKS
HEADS_HERE = 2
SCALE = HEAD_DIM ** (-0.5)
SCALE2 = SCALE * math.log2(math.e)
MESH = pl.DeviceIdType.MESH
BF16 = jnp.bfloat16
F32 = jnp.float32
ANY = pl.BlockSpec(memory_space=pl.ANY)
SMEM = pl.BlockSpec(memory_space=pltpu.SMEM)


def dot(a, b, contract):
    return lax.dot_general(a, b, ((contract[:1], contract[1:]), ((), ())), preferred_element_type=F32)


def wait_bytes(ref, sem):
    pltpu.make_async_copy(ref, ref, sem).wait()


def kernel(
    groups, members, offsets, tab, q, k, v, g, out_o, out_q, out_k, out_v,
    land, fetched, slots, back, parts, sends, tiles, peaks, sums, outs, logs, deltas,
    edge_q, edge_k, edge_v, own_q, own_k, own_v,
    in_send, in_recv, in_own, to_send, to_recv, ret_send, ret_recv, end_send, end_recv, end_own,
):
    b, u = lax.axis_index("blk"), lax.axis_index("ulysses")
    span = members
    side = b // (groups // 2)
    shift = members // 4

    def head_columns(member, h):
        owner = lax.rem(member + side * (shift * h), members)
        return pl.ds(pl.multiple_of((owner * HEADS_HERE + h) * HEAD_DIM, HEAD_DIM), HEAD_DIM)

    def across(t, h):
        to = lax.rem(b + t, groups)
        to_side = to // (groups // 2)
        return to, lax.rem(u + members + (side - to_side) * (shift * h), members)

    def entry(name, *index):
        at, shape = offsets[name]
        flat = 0
        for n, i in zip(shape, index):
            flat = flat * n + i
        return tab[at + flat]

    barrier = pltpu.get_barrier_semaphore()
    for t in range(1, members):
        pl.semaphore_signal(
            barrier, inc=1, device_id=(b, lax.rem(u + t, members)), device_id_type=MESH
        )
    for h in range(HEADS_HERE):
        for t in range(1, groups):
            pl.semaphore_signal(barrier, inc=1, device_id=across(t, h), device_id_type=MESH)
    pl.semaphore_wait(barrier, members - 1 + HEADS_HERE * (groups - 1))

    sources = (k, v, q, g)

    def spread(h, n):
        src, dst = sources[n], land[h][n]
        for t in range(1, members):
            to = lax.rem(u + t, members)
            pltpu.make_async_remote_copy(
                src_ref=src.at[:, head_columns(to, h)],
                dst_ref=dst.at[u],
                send_sem=in_send.at[h, n],
                recv_sem=in_recv.at[h, n],
                device_id=(b, to),
                device_id_type=MESH,
            ).start()
        pltpu.make_async_copy(src.at[:, head_columns(u, h)], dst.at[u], in_own.at[h, n]).start()

    def landed(h, n):
        dst = land[h][n]
        wait_bytes(dst.at[pl.ds(0, members - 1)], in_recv.at[h, n])
        wait_bytes(dst.at[0], in_own.at[h, n])

    def send_linked(h):
        for n in range(2):
            src, slot, dst = land[h][n], slots[h][n], fetched[h][n]
            for t in range(1, groups):
                to, there = across(t, h)
                for s in range(NEED):
                    slot[t, s] = src[entry("pick", to, s)]
                pltpu.make_async_remote_copy(
                    src_ref=slot.at[t],
                    dst_ref=dst.at[pl.ds(pl.multiple_of(b * NEED, NEED), NEED)],
                    send_sem=to_send.at[h, n],
                    recv_sem=to_recv.at[h, n],
                    device_id=(to, there),
                    device_id_type=MESH,
                ).start()

    def linked(h):
        for n in range(2):
            wait_bytes(fetched[h][n].at[pl.ds(0, (groups - 1) * NEED)], to_recv.at[h, n])

    def forward(h):
        kr, vr, qr, gr = land[h]
        fk, fv = fetched[h]
        peaks[EDGES] = jnp.full((BLOCK, 1), -1e30, F32)
        sums[EDGES] = jnp.zeros((BLOCK, 1), F32)
        outs[EDGES] = jnp.zeros((BLOCK, HEAD_DIM), F32)

        def cross(c, _):
            made = []
            for s in range(NEED):
                e = c * NEED + s
                slot = entry("slot", e)
                tile = dot(qr[entry("query", e)], fk[slot], (1, 1))
                peak = jnp.max(tile, axis=1, keepdims=True)
                raised = jnp.exp2((tile - peak) * SCALE2)
                total = jnp.sum(raised, axis=1, keepdims=True)
                made.append((e, tile, peak, total, dot(raised.astype(BF16), fv[slot], (1, 0))))
            for e, tile, peak, total, out in made:
                tiles[e], peaks[e], sums[e], outs[e] = tile, peak, total, out
            return 0

        lax.fori_loop(0, LINKS, cross, 0)
        own_k[h][...] = jnp.zeros(own_k[h].shape, F32)
        own_v[h][...] = jnp.zeros(own_v[h].shape, F32)

        def own(half, _):
            made = []
            for r in range(2):
                i = half * 2 + r
                start = jnp.clip(i - 1, 0, span - 3)
                column = lax.broadcasted_iota(jnp.int32, (BLOCK, 3 * BLOCK), 1) + start * BLOCK
                inside = (column >= (i - 1) * BLOCK) & (column < (i + 2) * BLOCK)
                qi, gi = qr[i], gr[i]
                kw = kr[pl.ds(start, 3)].reshape(3 * BLOCK, HEAD_DIM)
                vw = vr[pl.ds(start, 3)].reshape(3 * BLOCK, HEAD_DIM)
                scores = jnp.where(inside, dot(qi, kw, (1, 1)), -1e30)
                edges = [entry("edges", i, e) for e in range(LINKS)]
                peak = jnp.max(scores, axis=1, keepdims=True)
                for e in edges:
                    peak = jnp.maximum(peak, peaks[e])
                raised = jnp.exp2((scores - peak) * SCALE2)
                total = jnp.sum(raised, axis=1, keepdims=True)
                out = dot(raised.astype(BF16), vw, (1, 0))
                for e in edges:
                    factor = jnp.exp2((peaks[e] - peak) * SCALE2)
                    total = total + sums[e] * factor
                    out = out + outs[e] * factor
                inverse = 1.0 / total
                out = out * inverse
                delta = jnp.sum(gi.astype(F32) * out, axis=1, keepdims=True)
                prob = raised * inverse
                dscore = (prob * (dot(gi, vw, (1, 1)) - delta)).astype(BF16)
                made.append((
                    i, start, out.astype(BF16), peak * SCALE2 + jnp.log2(total), delta,
                    dot(dscore, kw, (1, 0)), dot(dscore, qi, (0, 0)), dot(prob.astype(BF16), gi, (0, 0)),
                ))
            for i, start, out, log, delta, grad_q, grad_k, grad_v in made:
                sends[h][0][i], logs[i], deltas[i], own_q[h][i] = out, log, delta, grad_q
                own_k[h][pl.ds(start, 3)] += grad_k.reshape(3, BLOCK, HEAD_DIM)
                own_v[h][pl.ds(start, 3)] += grad_v.reshape(3, BLOCK, HEAD_DIM)
            return 0

        lax.fori_loop(0, span // 2, own, 0)

    def backward(h):
        _, _, qr, gr = land[h]
        fk, fv = fetched[h]
        edge_q[EDGES] = jnp.zeros((BLOCK, HEAD_DIM), F32)

        def cross(c, _):
            made = []
            for s in range(NEED):
                e = c * NEED + s
                slot, i = entry("slot", e), entry("query", e)
                qi, gi = qr[i], gr[i]
                prob = jnp.exp2(tiles[e] * SCALE2 - logs[i])
                dscore = (prob * (dot(gi, fv[slot], (1, 1)) - deltas[i])).astype(BF16)
                made.append((
                    e, dot(dscore, fk[slot], (1, 0)), (dot(dscore, qi, (0, 0)) * SCALE).astype(BF16),
                    dot(prob.astype(BF16), gi, (0, 0)).astype(BF16),
                ))
            for e, grad_q, grad_k, grad_v in made:
                edge_q[e], edge_k[e], edge_v[e] = grad_q, grad_k, grad_v
            return 0

        lax.fori_loop(0, LINKS, cross, 0)

    def send_back(h):
        for n, made in enumerate((edge_k, edge_v)):
            part, dst = parts[h][n], back[h][n]
            for t in range(1, groups):
                to, there = across(t, h)
                for s in range(NEED):
                    part[t, s] = made[entry("edge", to, s)]
                pltpu.make_async_remote_copy(
                    src_ref=part.at[t],
                    dst_ref=dst.at[pl.ds(pl.multiple_of(b * NEED, NEED), NEED)],
                    send_sem=ret_send.at[h, n],
                    recv_sem=ret_recv.at[h, n],
                    device_id=(to, there),
                    device_id_type=MESH,
                ).start()

    results = (out_o, out_q, out_k, out_v)

    def finish(h, n):
        src, dst = sends[h][n], results[n].at[:, head_columns(u, h)]
        for t in range(1, members):
            to = lax.rem(u + t, members)
            pltpu.make_async_remote_copy(
                src_ref=src.at[to],
                dst_ref=dst,
                send_sem=end_send.at[h, n],
                recv_sem=end_recv.at[h, n],
                device_id=(b, to),
                device_id_type=MESH,
            ).start()
        pltpu.make_async_copy(src.at[u], dst, end_own.at[h, n]).start()

    def queries(h):
        def one(i, _):
            total = own_q[h][i]
            for e in range(LINKS):
                total = total + edge_q[entry("edges", i, e)]
            sends[h][1][i] = (total * SCALE).astype(BF16)
            return 0

        lax.fori_loop(0, span, one, 0)

    def keys(h):
        for n, (own_part, factor) in enumerate(((own_k[h], SCALE), (own_v[h], 1.0))):
            got = back[h][n]
            got[groups * NEED] = jnp.zeros((BLOCK, HEAD_DIM), BF16)
            wait_bytes(got.at[pl.ds(0, (groups - 1) * NEED)], ret_recv.at[h, n])

            def one(j, _):
                total = own_part[j] * factor
                for e in range(LINKS):
                    total = total + got[entry("back", j, e)].astype(F32)
                sends[h][2 + n][j] = total.astype(BF16)
                return 0

            lax.fori_loop(0, span, one, 0)
            finish(h, 2 + n)

    spread(0, 0)
    spread(0, 1)
    landed(0, 0)
    landed(0, 1)
    spread(0, 2)
    spread(0, 3)
    send_linked(0)
    landed(0, 2)
    landed(0, 3)
    spread(1, 0)
    spread(1, 1)
    linked(0)
    forward(0)
    finish(0, 0)
    landed(1, 0)
    landed(1, 1)
    spread(1, 2)
    spread(1, 3)
    send_linked(1)
    backward(0)
    send_back(0)
    queries(0)
    finish(0, 1)
    landed(1, 2)
    landed(1, 3)
    linked(1)
    forward(1)
    finish(1, 0)
    backward(1)
    send_back(1)
    keys(0)
    queries(1)
    finish(1, 1)
    keys(1)
    for h in range(HEADS_HERE):
        for n in range(2):
            wait_bytes(fetched[h][n].at[pl.ds(0, (groups - 1) * NEED)], to_send.at[h, n])
            wait_bytes(back[h][n].at[pl.ds(0, (groups - 1) * NEED)], ret_send.at[h, n])
        for n in range(4):
            most = land[h][n].at[pl.ds(0, members - 1)]
            wait_bytes(most, in_send.at[h, n])
            wait_bytes(most, end_send.at[h, n])
            wait_bytes(most, end_recv.at[h, n])
            wait_bytes(land[h][n].at[0], end_own.at[h, n])


def tables(block_mask, span, groups, group_id):
    rows = lax.dynamic_slice_in_dim(block_mask, group_id * span, span, 0)
    iota = lambda shape, axis: lax.broadcasted_iota(jnp.int32, shape, axis)
    cube = rows.reshape(span, groups, span) * (iota((span, groups, span), 1) != group_id)
    wanted = jnp.max(cube, axis=0)
    linked = jnp.max(wanted, axis=1)
    before = (iota((span, span), 0) < iota((span, span), 1)).astype(jnp.int32)
    before_c = (iota((groups, groups), 0) < iota((groups, groups), 1)).astype(jnp.int32)
    rank_in = jnp.sum(wanted[:, :, None] * before[None], axis=1)
    link = jnp.sum(linked[:, None] * before_c, axis=0)
    has = jnp.sum(cube, axis=2)
    slot_in = jnp.sum(cube * rank_in[None], axis=2)
    place = jnp.sum(has[:, :, None] * before_c[None], axis=1)
    rank_out = jnp.sum(has[:, None, :] * before[:, :, None], axis=0)
    partner = iota((span, groups), 1)
    spot = iota((span, groups), 0)
    chosen = has[:, :, None] * (place[:, :, None] == iota((span, groups, LINKS), 2))
    edges = jnp.sum(chosen * (link[None] * NEED + slot_in)[:, :, None], axis=1)
    returns = jnp.sum(chosen * (partner * NEED + rank_out)[:, :, None], axis=1)
    valid = iota((span, LINKS), 1) < jnp.sum(has, axis=1)[:, None]
    pick = jnp.sum(
        (has * spot)[:, :, None] * (rank_out[:, :, None] == iota((span, groups, NEED), 2)), axis=0
    )
    link_is = linked[:, None] * (link[:, None] == iota((groups, EDGES), 1) // NEED)
    slot = jnp.sum(link_is * (iota((groups, EDGES), 0) * NEED + iota((groups, EDGES), 1) % NEED), axis=0)
    number = link[None] * NEED + slot_in
    query = jnp.sum(
        (has * spot)[:, :, None] * (number[:, :, None] == iota((span, groups, EDGES), 2)), axis=(0, 1)
    )
    edge = jnp.minimum(link[:, None] * NEED + iota((groups, NEED), 1), EDGES - 1)
    named = {
        "pick": pick,
        "edge": edge,
        "slot": slot,
        "query": query,
        "edges": jnp.where(valid, edges, EDGES),
        "back": jnp.where(valid, returns, groups * NEED),
    }
    offsets, at = {}, 0
    for name, array in named.items():
        offsets[name] = (at, array.shape)
        at += array.size
    return jnp.concatenate([array.reshape(-1) for array in named.values()]), offsets


def shards(query_tokens, key_tokens, value_tokens, cotangent, block_mask):
    groups, members = lax.axis_size("blk"), lax.axis_size("ulysses")
    tokens, model = query_tokens.shape
    span = members * tokens // BLOCK
    table, offsets = tables(block_mask, span, groups, lax.axis_index("blk"))
    dma = pltpu.SemaphoreType.DMA
    blocks = lambda n, dtype: pltpu.VMEM((n, BLOCK, HEAD_DIM), dtype)
    column = lambda n: pltpu.VMEM((n, BLOCK, 1), F32)
    pairs = lambda: pltpu.VMEM((groups, NEED, BLOCK, HEAD_DIM), BF16)
    each = lambda n, make: [[make() for _ in range(n)] for _ in range(HEADS_HERE)]
    whole = jax.ShapeDtypeStruct((tokens, model), BF16)
    return pl.pallas_call(
        functools.partial(kernel, groups, members, offsets),
        out_shape=(whole,) * 4,
        in_specs=[SMEM] + [ANY] * 4,
        out_specs=(ANY,) * 4,
        scratch_shapes=[
            each(4, lambda: blocks(span, BF16)),
            each(2, lambda: blocks(groups * NEED, BF16)),
            each(2, pairs),
            each(2, lambda: blocks(groups * NEED + 1, BF16)),
            each(2, pairs),
            each(4, lambda: blocks(span, BF16)),
            blocks(EDGES, F32),
            column(EDGES + 1),
            column(EDGES + 1),
            blocks(EDGES + 1, F32),
            column(span),
            column(span),
            blocks(EDGES + 1, F32),
            blocks(EDGES, BF16),
            blocks(EDGES, BF16),
            [blocks(span, F32) for _ in range(HEADS_HERE)],
            [blocks(span, F32) for _ in range(HEADS_HERE)],
            [blocks(span, F32) for _ in range(HEADS_HERE)],
        ]
        + [dma((HEADS_HERE, n)) for n in (4, 4, 4, 2, 2, 2, 2, 4, 4, 4)],
        compiler_params=pltpu.CompilerParams(
            collective_id=0, has_side_effects=True, vmem_limit_bytes=56 * 2**20
        ),
        name="attention",
    )(table, query_tokens, key_tokens, value_tokens, cotangent)


def solution(mesh):
    placed = P(("blk", "ulysses"), None)
    return jax.shard_map(
        shards,
        mesh=mesh,
        in_specs=(placed,) * 4 + (P(),),
        out_specs=(placed,) * 4,
        check_vma=False,
    )
```

```python
import functools
import math

import jax
import jax.numpy as jnp
from jax import lax
from jax.experimental import pallas as pl
from jax.experimental.pallas import tpu as pltpu
from jax.sharding import PartitionSpec as P

HEAD_DIM = 128
BLOCK = 128
NEED = 2
LINKS = 7
EDGES = NEED * LINKS
HEADS_HERE = 2
SCALE = HEAD_DIM ** (-0.5)
SCALE2 = SCALE * math.log2(math.e)
MESH = pl.DeviceIdType.MESH
BF16 = jnp.bfloat16
F32 = jnp.float32
ANY = pl.BlockSpec(memory_space=pl.ANY)
SMEM = pl.BlockSpec(memory_space=pltpu.SMEM)


def dot(a, b, contract):
    return lax.dot_general(a, b, ((contract[:1], contract[1:]), ((), ())), preferred_element_type=F32)


def wait_bytes(ref, sem):
    pltpu.make_async_copy(ref, ref, sem).wait()


def kernel(
    groups, members, cap, offsets, tab, q, k, v, g, out_o, out_q, out_k, out_v,
    land, fetched, slots, relayed, crossing, crossed, back, parts, relay_parts, relay_back, returning,
    sends, tiles, peaks, sums, outs, logs, deltas, edge_q, edge_k, edge_v, own_q, own_k, own_v,
    in_send, in_recv, in_own, to_send, to_recv, over_send, over_recv, ret_send, ret_recv,
    mid_send, mid_recv, home_send, home_recv, end_send, end_recv, end_own,
):
    b, u = lax.axis_index("blk"), lax.axis_index("ulysses")
    span = members
    near = groups // 2
    side = b // near
    shift = members // 4
    mirror = lax.rem(b + near, groups)
    spot = lax.rem(b, near)

    def head_columns(member, h):
        owner = lax.rem(member + side * (shift * h), members)
        return pl.ds(pl.multiple_of((owner * HEADS_HERE + h) * HEAD_DIM, HEAD_DIM), HEAD_DIM)

    def opposite(h):
        return mirror, lax.rem(u + members + (2 * side - 1) * (shift * h), members)

    def neighbour(t):
        return lax.rem(spot + t, near)

    def pair(n):
        return pl.ds(pl.multiple_of(n * NEED, NEED), NEED)

    def entry(name, *index):
        at, shape = offsets[name]
        flat = 0
        for n, i in zip(shape, index):
            flat = flat * n + i
        return tab[at + flat]

    barrier = pltpu.get_barrier_semaphore()
    for t in range(1, members):
        pl.semaphore_signal(
            barrier, inc=1, device_id=(b, lax.rem(u + t, members)), device_id_type=MESH
        )
    for t in range(1, near):
        pl.semaphore_signal(
            barrier, inc=1, device_id=(side * near + neighbour(t), u), device_id_type=MESH
        )
    for h in range(HEADS_HERE):
        pl.semaphore_signal(barrier, inc=1, device_id=opposite(h), device_id_type=MESH)
    pl.semaphore_wait(barrier, members - 1 + near - 1 + HEADS_HERE)

    sources = (k, v, q, g)

    def spread(h, n):
        src, dst = sources[n], land[h][n]
        for t in range(1, members):
            to = lax.rem(u + t, members)
            pltpu.make_async_remote_copy(
                src_ref=src.at[:, head_columns(to, h)],
                dst_ref=dst.at[u],
                send_sem=in_send.at[h, n],
                recv_sem=in_recv.at[h, n],
                device_id=(b, to),
                device_id_type=MESH,
            ).start()
        pltpu.make_async_copy(src.at[:, head_columns(u, h)], dst.at[u], in_own.at[h, n]).start()

    def landed(h, n):
        dst = land[h][n]
        wait_bytes(dst.at[pl.ds(0, members - 1)], in_recv.at[h, n])
        wait_bytes(dst.at[0], in_own.at[h, n])

    def send(src, dst, to, send_sem, recv_sem):
        pltpu.make_async_remote_copy(
            src_ref=src, dst_ref=dst, send_sem=send_sem, recv_sem=recv_sem,
            device_id=to, device_id_type=MESH,
        ).start()

    def send_crossing(h):
        for n in range(2):
            for c in range(cap):
                crossing[h][n][c] = land[h][n][entry("cross", c)]
                send(crossing[h][n].at[c], crossed[h][n].at[c], opposite(h), over_send.at[h, n], over_recv.at[h, n])

    def send_linked(h):
        for n in range(2):
            slot = slots[h][n]
            for t in range(1, near):
                to = side * near + neighbour(t)
                for s in range(NEED):
                    slot[t, s] = land[h][n][entry("pick", to, s)]
                send(slot.at[t], fetched[h][n].at[pair(b)], (to, u), to_send.at[h, n], to_recv.at[h, n])

    def relay(h):
        for n in range(2):
            got, slot = crossed[h][n], relayed[h][n]
            wait_bytes(got, over_recv.at[h, n])
            for s in range(NEED):
                fetched[h][n][mirror * NEED + s] = got[entry("relay", spot, s)]
            for t in range(1, near):
                for s in range(NEED):
                    slot[t, s] = got[entry("relay", neighbour(t), s)]
                to = side * near + neighbour(t)
                send(slot.at[t], fetched[h][n].at[pair(mirror)], (to, u), to_send.at[h, n], to_recv.at[h, n])

    def linked(h):
        for n in range(2):
            wait_bytes(fetched[h][n].at[pl.ds(0, 2 * (near - 1) * NEED)], to_recv.at[h, n])

    def forward(h):
        kr, vr, qr, gr = land[h]
        fk, fv = fetched[h]
        peaks[EDGES] = jnp.full((BLOCK, 1), -1e30, F32)
        sums[EDGES] = jnp.zeros((BLOCK, 1), F32)
        outs[EDGES] = jnp.zeros((BLOCK, HEAD_DIM), F32)

        def cross(c, _):
            made = []
            for s in range(NEED):
                e = c * NEED + s
                slot = entry("slot", e)
                tile = dot(qr[entry("query", e)], fk[slot], (1, 1))
                peak = jnp.max(tile, axis=1, keepdims=True)
                raised = jnp.exp2((tile - peak) * SCALE2)
                total = jnp.sum(raised, axis=1, keepdims=True)
                made.append((e, tile, peak, total, dot(raised.astype(BF16), fv[slot], (1, 0))))
            for e, tile, peak, total, out in made:
                tiles[e], peaks[e], sums[e], outs[e] = tile, peak, total, out
            return 0

        lax.fori_loop(0, LINKS, cross, 0)
        own_k[h][...] = jnp.zeros(own_k[h].shape, F32)
        own_v[h][...] = jnp.zeros(own_v[h].shape, F32)

        def own(half, _):
            made = []
            for r in range(2):
                i = half * 2 + r
                start = jnp.clip(i - 1, 0, span - 3)
                column = lax.broadcasted_iota(jnp.int32, (BLOCK, 3 * BLOCK), 1) + start * BLOCK
                inside = (column >= (i - 1) * BLOCK) & (column < (i + 2) * BLOCK)
                qi, gi = qr[i], gr[i]
                kw = kr[pl.ds(start, 3)].reshape(3 * BLOCK, HEAD_DIM)
                vw = vr[pl.ds(start, 3)].reshape(3 * BLOCK, HEAD_DIM)
                scores = jnp.where(inside, dot(qi, kw, (1, 1)), -1e30)
                edges = [entry("edges", i, e) for e in range(LINKS)]
                peak = jnp.max(scores, axis=1, keepdims=True)
                for e in edges:
                    peak = jnp.maximum(peak, peaks[e])
                raised = jnp.exp2((scores - peak) * SCALE2)
                total = jnp.sum(raised, axis=1, keepdims=True)
                out = dot(raised.astype(BF16), vw, (1, 0))
                for e in edges:
                    factor = jnp.exp2((peaks[e] - peak) * SCALE2)
                    total = total + sums[e] * factor
                    out = out + outs[e] * factor
                inverse = 1.0 / total
                out = out * inverse
                delta = jnp.sum(gi.astype(F32) * out, axis=1, keepdims=True)
                prob = raised * inverse
                dscore = (prob * (dot(gi, vw, (1, 1)) - delta)).astype(BF16)
                made.append((
                    i, start, out.astype(BF16), peak * SCALE2 + jnp.log2(total), delta,
                    dot(dscore, kw, (1, 0)), dot(dscore, qi, (0, 0)), dot(prob.astype(BF16), gi, (0, 0)),
                ))
            for i, start, out, log, delta, grad_q, grad_k, grad_v in made:
                sends[h][0][i], logs[i], deltas[i], own_q[h][i] = out, log, delta, grad_q
                own_k[h][pl.ds(start, 3)] += grad_k.reshape(3, BLOCK, HEAD_DIM)
                own_v[h][pl.ds(start, 3)] += grad_v.reshape(3, BLOCK, HEAD_DIM)
            return 0

        lax.fori_loop(0, span // 2, own, 0)

    def backward(h):
        _, _, qr, gr = land[h]
        fk, fv = fetched[h]
        edge_q[EDGES] = jnp.zeros((BLOCK, HEAD_DIM), F32)

        def cross(c, _):
            made = []
            for s in range(NEED):
                e = c * NEED + s
                slot, i = entry("slot", e), entry("query", e)
                qi, gi = qr[i], gr[i]
                prob = jnp.exp2(tiles[e] * SCALE2 - logs[i])
                dscore = (prob * (dot(gi, fv[slot], (1, 1)) - deltas[i])).astype(BF16)
                made.append((
                    e, dot(dscore, fk[slot], (1, 0)), (dot(dscore, qi, (0, 0)) * SCALE).astype(BF16),
                    dot(prob.astype(BF16), gi, (0, 0)).astype(BF16),
                ))
            for e, grad_q, grad_k, grad_v in made:
                edge_q[e], edge_k[e], edge_v[e] = grad_q, grad_k, grad_v
            return 0

        lax.fori_loop(0, LINKS, cross, 0)

    def send_back(h):
        for n, made in enumerate((edge_k, edge_v)):
            part, relay_part = parts[h][n], relay_parts[h][n]
            for s in range(NEED):
                relay_back[h][n][spot * NEED + s] = made[entry("edge", mirror, s)]
            for t in range(1, near):
                to = neighbour(t)
                for s in range(NEED):
                    relay_part[t, s] = made[entry("edge", lax.rem(side + 1, 2) * near + to, s)]
                    part[t, s] = made[entry("edge", side * near + to, s)]
                there = (side * near + to, u)
                send(relay_part.at[t], relay_back[h][n].at[pair(spot)], there, mid_send.at[h, n], mid_recv.at[h, n])
                send(part.at[t], back[h][n].at[pair(spot)], there, ret_send.at[h, n], ret_recv.at[h, n])

    def relay_home(h):
        for n in range(2):
            got = relay_back[h][n]
            wait_bytes(got.at[pl.ds(0, (near - 1) * NEED)], mid_recv.at[h, n])
            for c in range(cap):
                returning[h][n][c] = got[entry("return", c)]
                send(
                    returning[h][n].at[c], back[h][n].at[near * NEED + c], opposite(h),
                    home_send.at[h, n], home_recv.at[h, n],
                )

    results = (out_o, out_q, out_k, out_v)

    def finish(h, n):
        src, dst = sends[h][n], results[n].at[:, head_columns(u, h)]
        for t in range(1, members):
            to = lax.rem(u + t, members)
            pltpu.make_async_remote_copy(
                src_ref=src.at[to],
                dst_ref=dst,
                send_sem=end_send.at[h, n],
                recv_sem=end_recv.at[h, n],
                device_id=(b, to),
                device_id_type=MESH,
            ).start()
        pltpu.make_async_copy(src.at[u], dst, end_own.at[h, n]).start()

    def queries(h):
        def one(i, _):
            total = own_q[h][i]
            for e in range(LINKS):
                total = total + edge_q[entry("edges", i, e)]
            sends[h][1][i] = (total * SCALE).astype(BF16)
            return 0

        lax.fori_loop(0, span, one, 0)

    def keys(h):
        for n, (own_part, factor) in enumerate(((own_k[h], SCALE), (own_v[h], 1.0))):
            got = back[h][n]
            got[near * NEED + cap] = jnp.zeros((BLOCK, HEAD_DIM), BF16)
            wait_bytes(got.at[pl.ds(0, (near - 1) * NEED)], ret_recv.at[h, n])
            wait_bytes(got.at[pl.ds(0, cap)], home_recv.at[h, n])

            def one(j, _):
                total = own_part[j] * factor
                for e in range(LINKS):
                    total = total + got[entry("back", j, e)].astype(F32)
                sends[h][2 + n][j] = total.astype(BF16)
                return 0

            lax.fori_loop(0, span, one, 0)
            finish(h, 2 + n)

    spread(0, 0)
    spread(0, 1)
    spread(1, 0)
    spread(1, 1)
    landed(0, 0)
    landed(0, 1)
    send_crossing(0)
    landed(1, 0)
    landed(1, 1)
    send_crossing(1)
    spread(0, 2)
    spread(0, 3)
    send_linked(0)
    send_linked(1)
    spread(1, 2)
    spread(1, 3)
    relay(0)
    relay(1)
    landed(0, 2)
    landed(0, 3)
    linked(0)
    forward(0)
    finish(0, 0)
    backward(0)
    send_back(0)
    queries(0)
    finish(0, 1)
    landed(1, 2)
    landed(1, 3)
    linked(1)
    forward(1)
    finish(1, 0)
    backward(1)
    send_back(1)
    relay_home(0)
    queries(1)
    finish(1, 1)
    relay_home(1)
    keys(0)
    keys(1)
    for h in range(HEADS_HERE):
        for n in range(2):
            most = fetched[h][n].at[pl.ds(0, (near - 1) * NEED)]
            wait_bytes(fetched[h][n].at[pl.ds(0, 2 * (near - 1) * NEED)], to_send.at[h, n])
            wait_bytes(most, mid_send.at[h, n])
            wait_bytes(most, ret_send.at[h, n])
            wait_bytes(crossing[h][n], over_send.at[h, n])
            wait_bytes(returning[h][n], home_send.at[h, n])
        for n in range(4):
            most = land[h][n].at[pl.ds(0, members - 1)]
            wait_bytes(most, in_send.at[h, n])
            wait_bytes(most, end_send.at[h, n])
            wait_bytes(most, end_recv.at[h, n])
            wait_bytes(land[h][n].at[0], end_own.at[h, n])


def tables(block_mask, span, groups, group_id, cap):
    near = groups // 2
    rows = lax.dynamic_slice_in_dim(block_mask, group_id * span, span, 0)
    mirror = (group_id + near) % groups
    other_rows = lax.dynamic_slice_in_dim(block_mask, mirror * span, span, 0)
    far_from = lambda who: (iota((1, groups), 1) // near != who // near).astype(jnp.int32)
    iota = lambda shape, axis: lax.broadcasted_iota(jnp.int32, shape, axis)
    cube = rows.reshape(span, groups, span) * (iota((span, groups, span), 1) != group_id)
    wanted = jnp.max(cube, axis=0)
    linked = jnp.max(wanted, axis=1)
    before = (iota((span, span), 0) < iota((span, span), 1)).astype(jnp.int32)
    before_c = (iota((groups, groups), 0) < iota((groups, groups), 1)).astype(jnp.int32)
    rank_in = jnp.sum(wanted[:, :, None] * before[None], axis=1)
    link = jnp.sum(linked[:, None] * before_c, axis=0)
    has = jnp.sum(cube, axis=2)
    slot_in = jnp.sum(cube * rank_in[None], axis=2)
    place = jnp.sum(has[:, :, None] * before_c[None], axis=1)
    rank_out = jnp.sum(has[:, None, :] * before[:, :, None], axis=0)
    partner = iota((span, groups), 1)
    spot = iota((span, groups), 0)
    chosen = has[:, :, None] * (place[:, :, None] == iota((span, groups, LINKS), 2))
    edges = jnp.sum(chosen * (link[None] * NEED + slot_in)[:, :, None], axis=1)
    far = far_from(group_id)
    far_has = has * far
    far_place = jnp.sum(jnp.sum(far_has, axis=0)[:, None] * before_c, axis=0)[None] + rank_out
    from_back = jnp.where(far > 0, near * NEED + far_place, partner % near * NEED + rank_out)
    returns = jnp.sum(chosen * from_back[:, :, None], axis=1)
    cross = jnp.sum(
        (far_has * spot)[:, :, None] * (far_place[:, :, None] == iota((span, groups, cap), 2)), axis=(0, 1)
    )
    other = jnp.sum(other_rows.reshape(span, groups, span), axis=(0, 2))[:, None] * far_from(mirror).reshape(groups, 1)
    other_place = jnp.sum(other * before_c, axis=0)[:, None] + iota((groups, NEED), 1)
    other_used = (iota((groups, NEED), 1) < other).astype(jnp.int32)
    toward = iota((groups, NEED), 0) % near
    relay = lax.dynamic_slice_in_dim(jnp.minimum(other_place, cap - 1), group_id // near * near, near, 0)
    give_back = jnp.sum(
        (other_used * (toward * NEED + iota((groups, NEED), 1)))[:, :, None]
        * (other_place[:, :, None] == iota((groups, NEED, cap), 2)),
        axis=(0, 1),
    )
    valid = iota((span, LINKS), 1) < jnp.sum(has, axis=1)[:, None]
    pick = jnp.sum(
        (has * spot)[:, :, None] * (rank_out[:, :, None] == iota((span, groups, NEED), 2)), axis=0
    )
    link_is = linked[:, None] * (link[:, None] == iota((groups, EDGES), 1) // NEED)
    slot = jnp.sum(link_is * (iota((groups, EDGES), 0) * NEED + iota((groups, EDGES), 1) % NEED), axis=0)
    number = link[None] * NEED + slot_in
    query = jnp.sum(
        (has * spot)[:, :, None] * (number[:, :, None] == iota((span, groups, EDGES), 2)), axis=(0, 1)
    )
    edge = jnp.minimum(link[:, None] * NEED + iota((groups, NEED), 1), EDGES - 1)
    named = {
        "pick": pick,
        "cross": cross,
        "relay": relay,
        "return": give_back,
        "edge": edge,
        "slot": slot,
        "query": query,
        "edges": jnp.where(valid, edges, EDGES),
        "back": jnp.where(valid, returns, near * NEED + cap),
    }
    offsets, at = {}, 0
    for name, array in named.items():
        offsets[name] = (at, array.shape)
        at += array.size
    return jnp.concatenate([array.reshape(-1) for array in named.values()]), offsets


def shards(query_tokens, key_tokens, value_tokens, cotangent, block_mask):
    groups, members = lax.axis_size("blk"), lax.axis_size("ulysses")
    tokens, model = query_tokens.shape
    span = members * tokens // BLOCK
    cap = EDGES
    near = groups // 2
    table, offsets = tables(block_mask, span, groups, lax.axis_index("blk"), cap)
    dma = pltpu.SemaphoreType.DMA
    blocks = lambda n, dtype: pltpu.VMEM((n, BLOCK, HEAD_DIM), dtype)
    column = lambda n: pltpu.VMEM((n, BLOCK, 1), F32)
    pairs = lambda: pltpu.VMEM((near, NEED, BLOCK, HEAD_DIM), BF16)
    each = lambda n, make: [[make() for _ in range(n)] for _ in range(HEADS_HERE)]
    whole = jax.ShapeDtypeStruct((tokens, model), BF16)
    return pl.pallas_call(
        functools.partial(kernel, groups, members, cap, offsets),
        out_shape=(whole,) * 4,
        in_specs=[SMEM] + [ANY] * 4,
        out_specs=(ANY,) * 4,
        scratch_shapes=[
            each(4, lambda: blocks(span, BF16)),
            each(2, lambda: blocks(groups * NEED, BF16)),
            each(2, pairs),
            each(2, pairs),
            each(2, lambda: blocks(cap, BF16)),
            each(2, lambda: blocks(cap, BF16)),
            each(2, lambda: blocks(near * NEED + cap + 1, BF16)),
            each(2, pairs),
            each(2, pairs),
            each(2, lambda: blocks(near * NEED, BF16)),
            each(2, lambda: blocks(cap, BF16)),
            each(4, lambda: blocks(span, BF16)),
            blocks(EDGES, F32),
            column(EDGES + 1),
            column(EDGES + 1),
            blocks(EDGES + 1, F32),
            column(span),
            column(span),
            blocks(EDGES + 1, F32),
            blocks(EDGES, BF16),
            blocks(EDGES, BF16),
            [blocks(span, F32) for _ in range(HEADS_HERE)],
            [blocks(span, F32) for _ in range(HEADS_HERE)],
            [blocks(span, F32) for _ in range(HEADS_HERE)],
        ]
        + [dma((HEADS_HERE, n)) for n in (4, 4, 4, 2, 2, 2, 2, 2, 2, 2, 2, 2, 2, 4, 4, 4)],
        compiler_params=pltpu.CompilerParams(
            collective_id=0, has_side_effects=True, vmem_limit_bytes=56 * 2**20
        ),
        name="attention",
    )(table, query_tokens, key_tokens, value_tokens, cotangent)


def solution(mesh):
    placed = P(("blk", "ulysses"), None)
    return jax.shard_map(
        shards,
        mesh=mesh,
        in_specs=(placed,) * 4 + (P(),),
        out_specs=(placed,) * 4,
        check_vma=False,
    )
```

```python
import functools
import math

import jax
import jax.numpy as jnp
from jax import lax
from jax.experimental import pallas as pl
from jax.experimental.pallas import tpu as pltpu
from jax.sharding import PartitionSpec as P

HEAD_DIM = 128
BLOCK = 128
NEED = 2
LINKS = 7
EDGES = NEED * LINKS
FEW = 8
HEADS_HERE = 2
SCALE = HEAD_DIM ** (-0.5)
SCALE2 = SCALE * math.log2(math.e)
MESH = pl.DeviceIdType.MESH
BF16 = jnp.bfloat16
F32 = jnp.float32
ANY = pl.BlockSpec(memory_space=pl.ANY)
SMEM = pl.BlockSpec(memory_space=pltpu.SMEM)


def dot(a, b, contract):
    return lax.dot_general(a, b, ((contract[:1], contract[1:]), ((), ())), preferred_element_type=F32)


def wait_bytes(ref, sem):
    pltpu.make_async_copy(ref, ref, sem).wait()


def kernel(
    groups, members, cap, offsets, tab, q, k, v, g, out_o, out_q, out_k, out_v,
    land, fetched, slots, relayed, crossing, crossed, back, parts, relay_parts, relay_back, returning,
    sends, tiles, peaks, sums, outs, logs, deltas, edge_q, edge_k, edge_v, own_q, own_k, own_v,
    in_send, in_recv, in_own, to_send, to_recv, over_send, over_recv, ret_send, ret_recv,
    mid_send, mid_recv, home_send, home_recv, end_send, end_recv, end_own,
):
    b, u = lax.axis_index("blk"), lax.axis_index("ulysses")
    span = members
    near = groups // 2
    side = b // near
    shift = members // 4
    mirror = lax.rem(b + near, groups)
    spot = lax.rem(b, near)

    def head_columns(member, h):
        owner = lax.rem(member + side * (shift * h), members)
        return pl.ds(pl.multiple_of((owner * HEADS_HERE + h) * HEAD_DIM, HEAD_DIM), HEAD_DIM)

    def opposite(h):
        return mirror, lax.rem(u + members + (2 * side - 1) * (shift * h), members)

    def neighbour(t):
        return lax.rem(spot + t, near)

    def pair(n):
        return pl.ds(pl.multiple_of(n * NEED, NEED), NEED)

    def entry(name, *index):
        at, shape = offsets[name]
        flat = 0
        for n, i in zip(shape, index):
            flat = flat * n + i
        return tab[at + flat]

    barrier = pltpu.get_barrier_semaphore()
    for t in range(1, members):
        pl.semaphore_signal(
            barrier, inc=1, device_id=(b, lax.rem(u + t, members)), device_id_type=MESH
        )
    for t in range(1, near):
        pl.semaphore_signal(
            barrier, inc=1, device_id=(side * near + neighbour(t), u), device_id_type=MESH
        )
    for h in range(HEADS_HERE):
        pl.semaphore_signal(barrier, inc=1, device_id=opposite(h), device_id_type=MESH)
    pl.semaphore_wait(barrier, members - 1 + near - 1 + HEADS_HERE)

    sources = (k, v, q, g)

    def spread(h, n):
        src, dst = sources[n], land[h][n]
        for t in range(1, members):
            to = lax.rem(u + t, members)
            pltpu.make_async_remote_copy(
                src_ref=src.at[:, head_columns(to, h)],
                dst_ref=dst.at[u],
                send_sem=in_send.at[h, n],
                recv_sem=in_recv.at[h, n],
                device_id=(b, to),
                device_id_type=MESH,
            ).start()
        pltpu.make_async_copy(src.at[:, head_columns(u, h)], dst.at[u], in_own.at[h, n]).start()

    def landed(h, n):
        dst = land[h][n]
        wait_bytes(dst.at[pl.ds(0, members - 1)], in_recv.at[h, n])
        wait_bytes(dst.at[0], in_own.at[h, n])

    def send(src, dst, to, send_sem, recv_sem):
        pltpu.make_async_remote_copy(
            src_ref=src, dst_ref=dst, send_sem=send_sem, recv_sem=recv_sem,
            device_id=to, device_id_type=MESH,
        ).start()

    def send_crossing(h):
        for n in range(2):
            for c in range(cap):
                crossing[h][n][c] = land[h][n][entry("cross", c)]
                send(crossing[h][n].at[c], crossed[h][n].at[c], opposite(h), over_send.at[h, n], over_recv.at[h, n])

    def send_linked(h):
        for n in range(2):
            slot = slots[h][n]
            for t in range(1, near):
                to = side * near + neighbour(t)
                for s in range(NEED):
                    slot[t, s] = land[h][n][entry("pick", to, s)]
                send(slot.at[t], fetched[h][n].at[pair(b)], (to, u), to_send.at[h, n], to_recv.at[h, n])

    def relay(h):
        for n in range(2):
            got, slot = crossed[h][n], relayed[h][n]
            wait_bytes(got, over_recv.at[h, n])
            for s in range(NEED):
                fetched[h][n][mirror * NEED + s] = got[jnp.minimum(entry("relay", spot, s), cap - 1)]
            for t in range(1, near):
                for s in range(NEED):
                    slot[t, s] = got[jnp.minimum(entry("relay", neighbour(t), s), cap - 1)]
                to = side * near + neighbour(t)
                send(slot.at[t], fetched[h][n].at[pair(mirror)], (to, u), to_send.at[h, n], to_recv.at[h, n])

    def linked(h):
        for n in range(2):
            wait_bytes(fetched[h][n].at[pl.ds(0, 2 * (near - 1) * NEED)], to_recv.at[h, n])

    def forward(h):
        kr, vr, qr, gr = land[h]
        fk, fv = fetched[h]
        peaks[EDGES] = jnp.full((BLOCK, 1), -1e30, F32)
        sums[EDGES] = jnp.zeros((BLOCK, 1), F32)
        outs[EDGES] = jnp.zeros((BLOCK, HEAD_DIM), F32)

        def cross(c, _):
            made = []
            for s in range(NEED):
                e = c * NEED + s
                slot = entry("slot", e)
                tile = dot(qr[entry("query", e)], fk[slot], (1, 1))
                peak = jnp.max(tile, axis=1, keepdims=True)
                raised = jnp.exp2((tile - peak) * SCALE2)
                total = jnp.sum(raised, axis=1, keepdims=True)
                made.append((e, tile, peak, total, dot(raised.astype(BF16), fv[slot], (1, 0))))
            for e, tile, peak, total, out in made:
                tiles[e], peaks[e], sums[e], outs[e] = tile, peak, total, out
            return 0

        lax.fori_loop(0, LINKS, cross, 0)
        own_k[h][...] = jnp.zeros(own_k[h].shape, F32)
        own_v[h][...] = jnp.zeros(own_v[h].shape, F32)

        def own(half, _):
            made = []
            for r in range(2):
                i = half * 2 + r
                start = jnp.clip(i - 1, 0, span - 3)
                column = lax.broadcasted_iota(jnp.int32, (BLOCK, 3 * BLOCK), 1) + start * BLOCK
                inside = (column >= (i - 1) * BLOCK) & (column < (i + 2) * BLOCK)
                qi, gi = qr[i], gr[i]
                kw = kr[pl.ds(start, 3)].reshape(3 * BLOCK, HEAD_DIM)
                vw = vr[pl.ds(start, 3)].reshape(3 * BLOCK, HEAD_DIM)
                scores = jnp.where(inside, dot(qi, kw, (1, 1)), -1e30)
                edges = [entry("edges", i, e) for e in range(LINKS)]
                peak = jnp.max(scores, axis=1, keepdims=True)
                for e in edges:
                    peak = jnp.maximum(peak, peaks[e])
                raised = jnp.exp2((scores - peak) * SCALE2)
                total = jnp.sum(raised, axis=1, keepdims=True)
                out = dot(raised.astype(BF16), vw, (1, 0))
                for e in edges:
                    factor = jnp.exp2((peaks[e] - peak) * SCALE2)
                    total = total + sums[e] * factor
                    out = out + outs[e] * factor
                inverse = 1.0 / total
                out = out * inverse
                delta = jnp.sum(gi.astype(F32) * out, axis=1, keepdims=True)
                prob = raised * inverse
                dscore = (prob * (dot(gi, vw, (1, 1)) - delta)).astype(BF16)
                made.append((
                    i, start, out.astype(BF16), peak * SCALE2 + jnp.log2(total), delta,
                    dot(dscore, kw, (1, 0)), dot(dscore, qi, (0, 0)), dot(prob.astype(BF16), gi, (0, 0)),
                ))
            for i, start, out, log, delta, grad_q, grad_k, grad_v in made:
                sends[h][0][i], logs[i], deltas[i], own_q[h][i] = out, log, delta, grad_q
                own_k[h][pl.ds(start, 3)] += grad_k.reshape(3, BLOCK, HEAD_DIM)
                own_v[h][pl.ds(start, 3)] += grad_v.reshape(3, BLOCK, HEAD_DIM)
            return 0

        lax.fori_loop(0, span // 2, own, 0)

    def backward(h):
        _, _, qr, gr = land[h]
        fk, fv = fetched[h]
        edge_q[EDGES] = jnp.zeros((BLOCK, HEAD_DIM), F32)

        def cross(c, _):
            made = []
            for s in range(NEED):
                e = c * NEED + s
                slot, i = entry("slot", e), entry("query", e)
                qi, gi = qr[i], gr[i]
                prob = jnp.exp2(tiles[e] * SCALE2 - logs[i])
                dscore = (prob * (dot(gi, fv[slot], (1, 1)) - deltas[i])).astype(BF16)
                made.append((
                    e, dot(dscore, fk[slot], (1, 0)), (dot(dscore, qi, (0, 0)) * SCALE).astype(BF16),
                    dot(prob.astype(BF16), gi, (0, 0)).astype(BF16),
                ))
            for e, grad_q, grad_k, grad_v in made:
                edge_q[e], edge_k[e], edge_v[e] = grad_q, grad_k, grad_v
            return 0

        lax.fori_loop(0, LINKS, cross, 0)

    def send_back(h):
        for n, made in enumerate((edge_k, edge_v)):
            part, relay_part = parts[h][n], relay_parts[h][n]
            for s in range(NEED):
                relay_back[h][n][spot * NEED + s] = made[entry("edge", mirror, s)]
            for t in range(1, near):
                to = neighbour(t)
                for s in range(NEED):
                    relay_part[t, s] = made[entry("edge", lax.rem(side + 1, 2) * near + to, s)]
                    part[t, s] = made[entry("edge", side * near + to, s)]
                there = (side * near + to, u)
                send(relay_part.at[t], relay_back[h][n].at[pair(spot)], there, mid_send.at[h, n], mid_recv.at[h, n])
                send(part.at[t], back[h][n].at[pair(spot)], there, ret_send.at[h, n], ret_recv.at[h, n])

    def relay_home(h):
        for n in range(2):
            got = relay_back[h][n]
            wait_bytes(got.at[pl.ds(0, (near - 1) * NEED)], mid_recv.at[h, n])
            for c in range(cap):
                returning[h][n][c] = got[entry("return", c)]
                send(
                    returning[h][n].at[c], back[h][n].at[near * NEED + c], opposite(h),
                    home_send.at[h, n], home_recv.at[h, n],
                )

    results = (out_o, out_q, out_k, out_v)

    def finish(h, n):
        src, dst = sends[h][n], results[n].at[:, head_columns(u, h)]
        for t in range(1, members):
            to = lax.rem(u + t, members)
            pltpu.make_async_remote_copy(
                src_ref=src.at[to],
                dst_ref=dst,
                send_sem=end_send.at[h, n],
                recv_sem=end_recv.at[h, n],
                device_id=(b, to),
                device_id_type=MESH,
            ).start()
        pltpu.make_async_copy(src.at[u], dst, end_own.at[h, n]).start()

    def queries(h):
        def one(i, _):
            total = own_q[h][i]
            for e in range(LINKS):
                total = total + edge_q[entry("edges", i, e)]
            sends[h][1][i] = (total * SCALE).astype(BF16)
            return 0

        lax.fori_loop(0, span, one, 0)

    def keys(h):
        for n, (own_part, factor) in enumerate(((own_k[h], SCALE), (own_v[h], 1.0))):
            got = back[h][n]
            got[near * NEED + EDGES] = jnp.zeros((BLOCK, HEAD_DIM), BF16)
            wait_bytes(got.at[pl.ds(0, (near - 1) * NEED)], ret_recv.at[h, n])
            wait_bytes(got.at[pl.ds(0, cap)], home_recv.at[h, n])

            def one(j, _):
                total = own_part[j] * factor
                for e in range(LINKS):
                    total = total + got[entry("back", j, e)].astype(F32)
                sends[h][2 + n][j] = total.astype(BF16)
                return 0

            lax.fori_loop(0, span, one, 0)
            finish(h, 2 + n)

    spread(0, 0)
    spread(0, 1)
    spread(1, 0)
    spread(1, 1)
    landed(0, 0)
    landed(0, 1)
    send_crossing(0)
    landed(1, 0)
    landed(1, 1)
    send_crossing(1)
    spread(0, 2)
    spread(0, 3)
    send_linked(0)
    send_linked(1)
    spread(1, 2)
    spread(1, 3)
    relay(0)
    relay(1)
    landed(0, 2)
    landed(0, 3)
    linked(0)
    forward(0)
    finish(0, 0)
    backward(0)
    send_back(0)
    queries(0)
    finish(0, 1)
    landed(1, 2)
    landed(1, 3)
    linked(1)
    forward(1)
    finish(1, 0)
    backward(1)
    send_back(1)
    relay_home(0)
    queries(1)
    finish(1, 1)
    relay_home(1)
    keys(0)
    keys(1)
    for h in range(HEADS_HERE):
        for n in range(2):
            most = fetched[h][n].at[pl.ds(0, (near - 1) * NEED)]
            wait_bytes(fetched[h][n].at[pl.ds(0, 2 * (near - 1) * NEED)], to_send.at[h, n])
            wait_bytes(most, mid_send.at[h, n])
            wait_bytes(most, ret_send.at[h, n])
            wait_bytes(crossing[h][n], over_send.at[h, n])
            wait_bytes(returning[h][n], home_send.at[h, n])
        for n in range(4):
            most = land[h][n].at[pl.ds(0, members - 1)]
            wait_bytes(most, in_send.at[h, n])
            wait_bytes(most, end_send.at[h, n])
            wait_bytes(most, end_recv.at[h, n])
            wait_bytes(land[h][n].at[0], end_own.at[h, n])


def tables(block_mask, span, groups, group_id):
    near = groups // 2
    rows = lax.dynamic_slice_in_dim(block_mask, group_id * span, span, 0)
    mirror = (group_id + near) % groups
    other_rows = lax.dynamic_slice_in_dim(block_mask, mirror * span, span, 0)
    far_from = lambda who: (iota((1, groups), 1) // near != who // near).astype(jnp.int32)
    iota = lambda shape, axis: lax.broadcasted_iota(jnp.int32, shape, axis)
    cube = rows.reshape(span, groups, span) * (iota((span, groups, span), 1) != group_id)
    wanted = jnp.max(cube, axis=0)
    linked = jnp.max(wanted, axis=1)
    before = (iota((span, span), 0) < iota((span, span), 1)).astype(jnp.int32)
    before_c = (iota((groups, groups), 0) < iota((groups, groups), 1)).astype(jnp.int32)
    rank_in = jnp.sum(wanted[:, :, None] * before[None], axis=1)
    link = jnp.sum(linked[:, None] * before_c, axis=0)
    has = jnp.sum(cube, axis=2)
    slot_in = jnp.sum(cube * rank_in[None], axis=2)
    place = jnp.sum(has[:, :, None] * before_c[None], axis=1)
    rank_out = jnp.sum(has[:, None, :] * before[:, :, None], axis=0)
    partner = iota((span, groups), 1)
    spot = iota((span, groups), 0)
    chosen = has[:, :, None] * (place[:, :, None] == iota((span, groups, LINKS), 2))
    edges = jnp.sum(chosen * (link[None] * NEED + slot_in)[:, :, None], axis=1)
    far = far_from(group_id)
    far_has = has * far
    far_place = jnp.sum(jnp.sum(far_has, axis=0)[:, None] * before_c, axis=0)[None] + rank_out
    from_back = jnp.where(far > 0, near * NEED + far_place, partner % near * NEED + rank_out)
    returns = jnp.sum(chosen * from_back[:, :, None], axis=1)
    cross = jnp.sum(
        (far_has * spot)[:, :, None] * (far_place[:, :, None] == iota((span, groups, EDGES), 2)), axis=(0, 1)
    )
    other = jnp.sum(other_rows.reshape(span, groups, span), axis=(0, 2))[:, None] * far_from(mirror).reshape(groups, 1)
    other_place = jnp.sum(other * before_c, axis=0)[:, None] + iota((groups, NEED), 1)
    other_used = (iota((groups, NEED), 1) < other).astype(jnp.int32)
    toward = iota((groups, NEED), 0) % near
    relay = lax.dynamic_slice_in_dim(other_place, group_id // near * near, near, 0)
    give_back = jnp.sum(
        (other_used * (toward * NEED + iota((groups, NEED), 1)))[:, :, None]
        * (other_place[:, :, None] == iota((groups, NEED, EDGES), 2)),
        axis=(0, 1),
    )
    valid = iota((span, LINKS), 1) < jnp.sum(has, axis=1)[:, None]
    pick = jnp.sum(
        (has * spot)[:, :, None] * (rank_out[:, :, None] == iota((span, groups, NEED), 2)), axis=0
    )
    link_is = linked[:, None] * (link[:, None] == iota((groups, EDGES), 1) // NEED)
    slot = jnp.sum(link_is * (iota((groups, EDGES), 0) * NEED + iota((groups, EDGES), 1) % NEED), axis=0)
    number = link[None] * NEED + slot_in
    query = jnp.sum(
        (has * spot)[:, :, None] * (number[:, :, None] == iota((span, groups, EDGES), 2)), axis=(0, 1)
    )
    edge = jnp.minimum(link[:, None] * NEED + iota((groups, NEED), 1), EDGES - 1)
    named = {
        "pick": pick,
        "cross": cross,
        "relay": relay,
        "return": give_back,
        "edge": edge,
        "slot": slot,
        "query": query,
        "edges": jnp.where(valid, edges, EDGES),
        "back": jnp.where(valid, returns, near * NEED + EDGES),
    }
    offsets, at = {}, 0
    for name, array in named.items():
        offsets[name] = (at, array.shape)
        at += array.size
    return jnp.concatenate([array.reshape(-1) for array in named.values()]), offsets


def most_crossing(block_mask, span, groups):
    blocks = block_mask.shape[0]
    iota = lambda shape, axis: lax.broadcasted_iota(jnp.int32, shape, axis)
    side = lambda axis: iota(block_mask.shape, axis) // (blocks // 2)
    rows = jnp.sum(jnp.where(side(0) != side(1), block_mask, 0), axis=1, keepdims=True)
    belongs = iota((blocks, groups), 0) // span == iota((blocks, groups), 1)
    return jnp.max(jnp.sum(jnp.where(belongs, rows, 0), axis=0))


def shards(query_tokens, key_tokens, value_tokens, cotangent, block_mask):
    groups, members = lax.axis_size("blk"), lax.axis_size("ulysses")
    tokens, model = query_tokens.shape
    span = members * tokens // BLOCK
    near = groups // 2
    table, offsets = tables(block_mask, span, groups, lax.axis_index("blk"))
    dma = pltpu.SemaphoreType.DMA
    blocks = lambda n, dtype: pltpu.VMEM((n, BLOCK, HEAD_DIM), dtype)
    column = lambda n: pltpu.VMEM((n, BLOCK, 1), F32)
    pairs = lambda: pltpu.VMEM((near, NEED, BLOCK, HEAD_DIM), BF16)
    each = lambda n, make: [[make() for _ in range(n)] for _ in range(HEADS_HERE)]
    whole = jax.ShapeDtypeStruct((tokens, model), BF16)
    call = lambda cap, name, collective_id: pl.pallas_call(
        functools.partial(kernel, groups, members, cap, offsets),
        out_shape=(whole,) * 4,
        in_specs=[SMEM] + [ANY] * 4,
        out_specs=(ANY,) * 4,
        scratch_shapes=[
            each(4, lambda: blocks(span, BF16)),
            each(2, lambda: blocks(groups * NEED, BF16)),
            each(2, pairs),
            each(2, pairs),
            each(2, lambda: blocks(cap, BF16)),
            each(2, lambda: blocks(cap, BF16)),
            each(2, lambda: blocks(near * NEED + EDGES + 1, BF16)),
            each(2, pairs),
            each(2, pairs),
            each(2, lambda: blocks(near * NEED, BF16)),
            each(2, lambda: blocks(cap, BF16)),
            each(4, lambda: blocks(span, BF16)),
            blocks(EDGES, F32),
            column(EDGES + 1),
            column(EDGES + 1),
            blocks(EDGES + 1, F32),
            column(span),
            column(span),
            blocks(EDGES + 1, F32),
            blocks(EDGES, BF16),
            blocks(EDGES, BF16),
            [blocks(span, F32) for _ in range(HEADS_HERE)],
            [blocks(span, F32) for _ in range(HEADS_HERE)],
            [blocks(span, F32) for _ in range(HEADS_HERE)],
        ]
        + [dma((HEADS_HERE, n)) for n in (4, 4, 4, 2, 2, 2, 2, 2, 2, 2, 2, 2, 2, 4, 4, 4)],
        compiler_params=pltpu.CompilerParams(
            collective_id=collective_id, has_side_effects=True, vmem_limit_bytes=56 * 2**20
        ),
        name=name,
    )
    return lax.cond(
        most_crossing(block_mask, span, groups) <= FEW,
        call(FEW, "attention_few", 0),
        call(EDGES, "attention_most", 1),
        table, query_tokens, key_tokens, value_tokens, cotangent,
    )


def solution(mesh):
    placed = P(("blk", "ulysses"), None)
    return jax.shard_map(
        shards,
        mesh=mesh,
        in_specs=(placed,) * 4 + (P(),),
        out_specs=(placed,) * 4,
        check_vma=False,
    )
```

```python
import functools
import math

import jax
import jax.numpy as jnp
from jax import lax
from jax.experimental import pallas as pl
from jax.experimental.pallas import tpu as pltpu
from jax.sharding import PartitionSpec as P

HEAD_DIM = 128
BLOCK = 128
NEED = 2
LINKS = 7
EDGES = NEED * LINKS
FEW = 8
HEADS_HERE = 2
SCALE = HEAD_DIM ** (-0.5)
SCALE2 = SCALE * math.log2(math.e)
MESH = pl.DeviceIdType.MESH
BF16 = jnp.bfloat16
F32 = jnp.float32
ANY = pl.BlockSpec(memory_space=pl.ANY)
SMEM = pl.BlockSpec(memory_space=pltpu.SMEM)


def dot(a, b, contract):
    return lax.dot_general(a, b, ((contract[:1], contract[1:]), ((), ())), preferred_element_type=F32)


def wait_bytes(ref, sem):
    pltpu.make_async_copy(ref, ref, sem).wait()


def kernel(
    groups, members, cap, offsets, tab, q, k, v, g, out_o, out_q, out_k, out_v,
    land, fetched, slots, relayed, crossing, crossed, back, parts, relay_parts, relay_back, returning,
    sends, tiles, peaks, sums, outs, logs, deltas, edge_q, edge_k, edge_v, own_k, own_v, probs,
    in_send, in_recv, in_own, to_send, to_recv, over_send, over_recv, ret_send, ret_recv,
    mid_send, mid_recv, home_send, home_recv, end_send, end_recv, end_own,
):
    b, u = lax.axis_index("blk"), lax.axis_index("ulysses")
    span = members
    near = groups // 2
    side = b // near
    shift = members // 4
    mirror = lax.rem(b + near, groups)
    spot = lax.rem(b, near)

    def head_columns(member, h):
        owner = lax.rem(member + side * (shift * h), members)
        return pl.ds(pl.multiple_of((owner * HEADS_HERE + h) * HEAD_DIM, HEAD_DIM), HEAD_DIM)

    def opposite(h):
        return mirror, lax.rem(u + members + (2 * side - 1) * (shift * h), members)

    def neighbour(t):
        return lax.rem(spot + t, near)

    def pair(n):
        return pl.ds(pl.multiple_of(n * NEED, NEED), NEED)

    def entry(name, *index):
        at, shape = offsets[name]
        flat = 0
        for n, i in zip(shape, index):
            flat = flat * n + i
        return tab[at + flat]

    barrier = pltpu.get_barrier_semaphore()
    for t in range(1, members):
        pl.semaphore_signal(
            barrier, inc=1, device_id=(b, lax.rem(u + t, members)), device_id_type=MESH
        )
    for t in range(1, near):
        pl.semaphore_signal(
            barrier, inc=1, device_id=(side * near + neighbour(t), u), device_id_type=MESH
        )
    for h in range(HEADS_HERE):
        pl.semaphore_signal(barrier, inc=1, device_id=opposite(h), device_id_type=MESH)
    pl.semaphore_wait(barrier, members - 1 + near - 1 + HEADS_HERE)

    sources = (k, v, q, g)

    def spread(h, n):
        src, dst = sources[n], land[h][n]
        for t in range(1, members):
            to = lax.rem(u + t, members)
            pltpu.make_async_remote_copy(
                src_ref=src.at[:, head_columns(to, h)],
                dst_ref=dst.at[u],
                send_sem=in_send.at[h, n],
                recv_sem=in_recv.at[h, n],
                device_id=(b, to),
                device_id_type=MESH,
            ).start()
        pltpu.make_async_copy(src.at[:, head_columns(u, h)], dst.at[u], in_own.at[h, n]).start()

    def landed(h, n):
        dst = land[h][n]
        wait_bytes(dst.at[pl.ds(0, members - 1)], in_recv.at[h, n])
        wait_bytes(dst.at[0], in_own.at[h, n])

    def send(src, dst, to, send_sem, recv_sem):
        pltpu.make_async_remote_copy(
            src_ref=src, dst_ref=dst, send_sem=send_sem, recv_sem=recv_sem,
            device_id=to, device_id_type=MESH,
        ).start()

    def send_crossing(h):
        for n in range(2):
            for c in range(cap):
                crossing[h][n][c] = land[h][n][entry("cross", c)]
                send(crossing[h][n].at[c], crossed[h][n].at[c], opposite(h), over_send.at[h, n], over_recv.at[h, n])

    def send_linked(h):
        for n in range(2):
            slot = slots[h][n]
            for t in range(1, near):
                to = side * near + neighbour(t)
                for s in range(NEED):
                    slot[t, s] = land[h][n][entry("pick", to, s)]
                send(slot.at[t], fetched[h][n].at[pair(b)], (to, u), to_send.at[h, n], to_recv.at[h, n])

    def relay(h):
        for n in range(2):
            got, slot = crossed[h][n], relayed[h][n]
            wait_bytes(got, over_recv.at[h, n])
            for s in range(NEED):
                fetched[h][n][mirror * NEED + s] = got[jnp.minimum(entry("relay", spot, s), cap - 1)]
            for t in range(1, near):
                for s in range(NEED):
                    slot[t, s] = got[jnp.minimum(entry("relay", neighbour(t), s), cap - 1)]
                to = side * near + neighbour(t)
                send(slot.at[t], fetched[h][n].at[pair(mirror)], (to, u), to_send.at[h, n], to_recv.at[h, n])

    def linked(h):
        for n in range(2):
            wait_bytes(fetched[h][n].at[pl.ds(0, 2 * (near - 1) * NEED)], to_recv.at[h, n])

    def forward(h):
        kr, vr, qr, gr = land[h]
        fk, fv = fetched[h]
        peaks[EDGES] = jnp.full((BLOCK, 1), -1e30, F32)
        sums[EDGES] = jnp.zeros((BLOCK, 1), F32)
        outs[EDGES] = jnp.zeros((BLOCK, HEAD_DIM), F32)

        def cross(c, _):
            made = []
            for s in range(NEED):
                e = c * NEED + s
                slot = entry("slot", e)
                tile = dot(qr[entry("query", e)], fk[slot], (1, 1))
                peak = jnp.max(tile, axis=1, keepdims=True)
                raised = jnp.exp2((tile - peak) * SCALE2)
                total = jnp.sum(raised, axis=1, keepdims=True)
                made.append((e, tile, peak, total, dot(raised.astype(BF16), fv[slot], (1, 0))))
            for e, tile, peak, total, out in made:
                tiles[e], peaks[e], sums[e], outs[e] = tile, peak, total, out
            return 0

        lax.fori_loop(0, LINKS, cross, 0)

        def own(half, _):
            made = []
            for r in range(2):
                i = half * 2 + r
                start = jnp.clip(i - 1, 0, span - 3)
                column = lax.broadcasted_iota(jnp.int32, (BLOCK, 3 * BLOCK), 1) + start * BLOCK
                inside = (column >= (i - 1) * BLOCK) & (column < (i + 2) * BLOCK)
                qi, gi = qr[i], gr[i]
                kw = kr[pl.ds(start, 3)].reshape(3 * BLOCK, HEAD_DIM)
                vw = vr[pl.ds(start, 3)].reshape(3 * BLOCK, HEAD_DIM)
                scores = jnp.where(inside, dot(qi, kw, (1, 1)), -1e30)
                edges = [entry("edges", i, e) for e in range(LINKS)]
                peak = jnp.max(scores, axis=1, keepdims=True)
                for e in edges:
                    peak = jnp.maximum(peak, peaks[e])
                raised = jnp.exp2((scores - peak) * SCALE2)
                total = jnp.sum(raised, axis=1, keepdims=True)
                out = dot(raised.astype(BF16), vw, (1, 0))
                for e in edges:
                    factor = jnp.exp2((peaks[e] - peak) * SCALE2)
                    total = total + sums[e] * factor
                    out = out + outs[e] * factor
                inverse = 1.0 / total
                out = out * inverse
                delta = jnp.sum(gi.astype(F32) * out, axis=1, keepdims=True)
                made.append((i, out.astype(BF16), peak * SCALE2 + jnp.log2(total), delta, raised * inverse))
            for i, out, log, delta, prob in made:
                sends[h][0][i], logs[h][i], deltas[h][i], probs[h][i] = out, log, delta, prob
            return 0

        lax.fori_loop(0, span // 2, own, 0)

    def own_backward(h):
        kr, vr, qr, gr = land[h]
        own_k[h][...] = jnp.zeros(own_k[h].shape, F32)
        own_v[h][...] = jnp.zeros(own_v[h].shape, F32)

        def own(half, _):
            made = []
            for r in range(2):
                i = half * 2 + r
                start = jnp.clip(i - 1, 0, span - 3)
                qi, gi = qr[i], gr[i]
                kw = kr[pl.ds(start, 3)].reshape(3 * BLOCK, HEAD_DIM)
                vw = vr[pl.ds(start, 3)].reshape(3 * BLOCK, HEAD_DIM)
                prob = probs[h][i]
                dscore = (prob * (dot(gi, vw, (1, 1)) - deltas[h][i])).astype(BF16)
                grad_q = dot(dscore, kw, (1, 0))
                for e in range(LINKS):
                    grad_q = grad_q + edge_q[h][entry("edges", i, e)]
                made.append((
                    i, start, (grad_q * SCALE).astype(BF16),
                    dot(dscore, qi, (0, 0)), dot(prob.astype(BF16), gi, (0, 0)),
                ))
            for i, start, grad_q, grad_k, grad_v in made:
                sends[h][1][i] = grad_q
                own_k[h][pl.ds(start, 3)] += grad_k.reshape(3, BLOCK, HEAD_DIM)
                own_v[h][pl.ds(start, 3)] += grad_v.reshape(3, BLOCK, HEAD_DIM)
            return 0

        lax.fori_loop(0, span // 2, own, 0)

    def backward(h):
        _, _, qr, gr = land[h]
        fk, fv = fetched[h]
        edge_q[h][EDGES] = jnp.zeros((BLOCK, HEAD_DIM), F32)

        def cross(c, _):
            made = []
            for s in range(NEED):
                e = c * NEED + s
                slot, i = entry("slot", e), entry("query", e)
                qi, gi = qr[i], gr[i]
                prob = jnp.exp2(tiles[e] * SCALE2 - logs[h][i])
                dscore = (prob * (dot(gi, fv[slot], (1, 1)) - deltas[h][i])).astype(BF16)
                made.append((
                    e, dot(dscore, fk[slot], (1, 0)), (dot(dscore, qi, (0, 0)) * SCALE).astype(BF16),
                    dot(prob.astype(BF16), gi, (0, 0)).astype(BF16),
                ))
            for e, grad_q, grad_k, grad_v in made:
                edge_q[h][e], edge_k[e], edge_v[e] = grad_q, grad_k, grad_v
            return 0

        lax.fori_loop(0, LINKS, cross, 0)

    def send_back(h):
        for n, made in enumerate((edge_k, edge_v)):
            part, relay_part = parts[h][n], relay_parts[h][n]
            for s in range(NEED):
                relay_back[h][n][spot * NEED + s] = made[entry("edge", mirror, s)]
            for t in range(1, near):
                to = neighbour(t)
                for s in range(NEED):
                    relay_part[t, s] = made[entry("edge", lax.rem(side + 1, 2) * near + to, s)]
                    part[t, s] = made[entry("edge", side * near + to, s)]
                there = (side * near + to, u)
                send(relay_part.at[t], relay_back[h][n].at[pair(spot)], there, mid_send.at[h, n], mid_recv.at[h, n])
                send(part.at[t], back[h][n].at[pair(spot)], there, ret_send.at[h, n], ret_recv.at[h, n])

    def relay_home(h):
        for n in range(2):
            got = relay_back[h][n]
            wait_bytes(got.at[pl.ds(0, (near - 1) * NEED)], mid_recv.at[h, n])
            for c in range(cap):
                returning[h][n][c] = got[entry("return", c)]
                send(
                    returning[h][n].at[c], back[h][n].at[near * NEED + c], opposite(h),
                    home_send.at[h, n], home_recv.at[h, n],
                )

    results = (out_o, out_q, out_k, out_v)

    def finish(h, n):
        src, dst = sends[h][n], results[n].at[:, head_columns(u, h)]
        for t in range(1, members):
            to = lax.rem(u + t, members)
            pltpu.make_async_remote_copy(
                src_ref=src.at[to],
                dst_ref=dst,
                send_sem=end_send.at[h, n],
                recv_sem=end_recv.at[h, n],
                device_id=(b, to),
                device_id_type=MESH,
            ).start()
        pltpu.make_async_copy(src.at[u], dst, end_own.at[h, n]).start()

    def keys(h):
        for n, (own_part, factor) in enumerate(((own_k[h], SCALE), (own_v[h], 1.0))):
            got = back[h][n]
            got[near * NEED + EDGES] = jnp.zeros((BLOCK, HEAD_DIM), BF16)
            wait_bytes(got.at[pl.ds(0, (near - 1) * NEED)], ret_recv.at[h, n])
            wait_bytes(got.at[pl.ds(0, cap)], home_recv.at[h, n])

            def one(j, _):
                total = own_part[j] * factor
                for e in range(LINKS):
                    total = total + got[entry("back", j, e)].astype(F32)
                sends[h][2 + n][j] = total.astype(BF16)
                return 0

            lax.fori_loop(0, span, one, 0)
            finish(h, 2 + n)

    spread(0, 0)
    spread(0, 1)
    spread(1, 0)
    spread(1, 1)
    landed(0, 0)
    landed(0, 1)
    send_crossing(0)
    landed(1, 0)
    landed(1, 1)
    send_crossing(1)
    spread(0, 2)
    spread(0, 3)
    send_linked(0)
    send_linked(1)
    spread(1, 2)
    spread(1, 3)
    relay(0)
    relay(1)
    landed(0, 2)
    landed(0, 3)
    linked(0)
    forward(0)
    finish(0, 0)
    backward(0)
    send_back(0)
    own_backward(0)
    finish(0, 1)
    landed(1, 2)
    landed(1, 3)
    linked(1)
    forward(1)
    finish(1, 0)
    backward(1)
    send_back(1)
    relay_home(0)
    relay_home(1)
    keys(0)
    own_backward(1)
    finish(1, 1)
    keys(1)
    for h in range(HEADS_HERE):
        for n in range(2):
            most = fetched[h][n].at[pl.ds(0, (near - 1) * NEED)]
            wait_bytes(fetched[h][n].at[pl.ds(0, 2 * (near - 1) * NEED)], to_send.at[h, n])
            wait_bytes(most, mid_send.at[h, n])
            wait_bytes(most, ret_send.at[h, n])
            wait_bytes(crossing[h][n], over_send.at[h, n])
            wait_bytes(returning[h][n], home_send.at[h, n])
        for n in range(4):
            most = land[h][n].at[pl.ds(0, members - 1)]
            wait_bytes(most, in_send.at[h, n])
            wait_bytes(most, end_send.at[h, n])
            wait_bytes(most, end_recv.at[h, n])
            wait_bytes(land[h][n].at[0], end_own.at[h, n])


def tables(block_mask, span, groups, group_id):
    near = groups // 2
    rows = lax.dynamic_slice_in_dim(block_mask, group_id * span, span, 0)
    mirror = (group_id + near) % groups
    other_rows = lax.dynamic_slice_in_dim(block_mask, mirror * span, span, 0)
    far_from = lambda who: (iota((1, groups), 1) // near != who // near).astype(jnp.int32)
    iota = lambda shape, axis: lax.broadcasted_iota(jnp.int32, shape, axis)
    cube = rows.reshape(span, groups, span) * (iota((span, groups, span), 1) != group_id)
    wanted = jnp.max(cube, axis=0)
    linked = jnp.max(wanted, axis=1)
    before = (iota((span, span), 0) < iota((span, span), 1)).astype(jnp.int32)
    before_c = (iota((groups, groups), 0) < iota((groups, groups), 1)).astype(jnp.int32)
    rank_in = jnp.sum(wanted[:, :, None] * before[None], axis=1)
    link = jnp.sum(linked[:, None] * before_c, axis=0)
    has = jnp.sum(cube, axis=2)
    slot_in = jnp.sum(cube * rank_in[None], axis=2)
    place = jnp.sum(has[:, :, None] * before_c[None], axis=1)
    rank_out = jnp.sum(has[:, None, :] * before[:, :, None], axis=0)
    partner = iota((span, groups), 1)
    spot = iota((span, groups), 0)
    chosen = has[:, :, None] * (place[:, :, None] == iota((span, groups, LINKS), 2))
    edges = jnp.sum(chosen * (link[None] * NEED + slot_in)[:, :, None], axis=1)
    far = far_from(group_id)
    far_has = has * far
    far_place = jnp.sum(jnp.sum(far_has, axis=0)[:, None] * before_c, axis=0)[None] + rank_out
    from_back = jnp.where(far > 0, near * NEED + far_place, partner % near * NEED + rank_out)
    returns = jnp.sum(chosen * from_back[:, :, None], axis=1)
    cross = jnp.sum(
        (far_has * spot)[:, :, None] * (far_place[:, :, None] == iota((span, groups, EDGES), 2)), axis=(0, 1)
    )
    other = jnp.sum(other_rows.reshape(span, groups, span), axis=(0, 2))[:, None] * far_from(mirror).reshape(groups, 1)
    other_place = jnp.sum(other * before_c, axis=0)[:, None] + iota((groups, NEED), 1)
    other_used = (iota((groups, NEED), 1) < other).astype(jnp.int32)
    toward = iota((groups, NEED), 0) % near
    relay = lax.dynamic_slice_in_dim(other_place, group_id // near * near, near, 0)
    give_back = jnp.sum(
        (other_used * (toward * NEED + iota((groups, NEED), 1)))[:, :, None]
        * (other_place[:, :, None] == iota((groups, NEED, EDGES), 2)),
        axis=(0, 1),
    )
    valid = iota((span, LINKS), 1) < jnp.sum(has, axis=1)[:, None]
    pick = jnp.sum(
        (has * spot)[:, :, None] * (rank_out[:, :, None] == iota((span, groups, NEED), 2)), axis=0
    )
    link_is = linked[:, None] * (link[:, None] == iota((groups, EDGES), 1) // NEED)
    slot = jnp.sum(link_is * (iota((groups, EDGES), 0) * NEED + iota((groups, EDGES), 1) % NEED), axis=0)
    number = link[None] * NEED + slot_in
    query = jnp.sum(
        (has * spot)[:, :, None] * (number[:, :, None] == iota((span, groups, EDGES), 2)), axis=(0, 1)
    )
    edge = jnp.minimum(link[:, None] * NEED + iota((groups, NEED), 1), EDGES - 1)
    named = {
        "pick": pick,
        "cross": cross,
        "relay": relay,
        "return": give_back,
        "edge": edge,
        "slot": slot,
        "query": query,
        "edges": jnp.where(valid, edges, EDGES),
        "back": jnp.where(valid, returns, near * NEED + EDGES),
    }
    offsets, at = {}, 0
    for name, array in named.items():
        offsets[name] = (at, array.shape)
        at += array.size
    return jnp.concatenate([array.reshape(-1) for array in named.values()]), offsets


def most_crossing(block_mask, span, groups):
    blocks = block_mask.shape[0]
    iota = lambda shape, axis: lax.broadcasted_iota(jnp.int32, shape, axis)
    side = lambda axis: iota(block_mask.shape, axis) // (blocks // 2)
    rows = jnp.sum(jnp.where(side(0) != side(1), block_mask, 0), axis=1, keepdims=True)
    belongs = iota((blocks, groups), 0) // span == iota((blocks, groups), 1)
    return jnp.max(jnp.sum(jnp.where(belongs, rows, 0), axis=0))


def shards(query_tokens, key_tokens, value_tokens, cotangent, block_mask):
    groups, members = lax.axis_size("blk"), lax.axis_size("ulysses")
    tokens, model = query_tokens.shape
    span = members * tokens // BLOCK
    near = groups // 2
    table, offsets = tables(block_mask, span, groups, lax.axis_index("blk"))
    dma = pltpu.SemaphoreType.DMA
    blocks = lambda n, dtype: pltpu.VMEM((n, BLOCK, HEAD_DIM), dtype)
    column = lambda n: pltpu.VMEM((n, BLOCK, 1), F32)
    pairs = lambda: pltpu.VMEM((near, NEED, BLOCK, HEAD_DIM), BF16)
    each = lambda n, make: [[make() for _ in range(n)] for _ in range(HEADS_HERE)]
    whole = jax.ShapeDtypeStruct((tokens, model), BF16)
    call = lambda cap, name, collective_id: pl.pallas_call(
        functools.partial(kernel, groups, members, cap, offsets),
        out_shape=(whole,) * 4,
        in_specs=[SMEM] + [ANY] * 4,
        out_specs=(ANY,) * 4,
        scratch_shapes=[
            each(4, lambda: blocks(span, BF16)),
            each(2, lambda: blocks(groups * NEED, BF16)),
            each(2, pairs),
            each(2, pairs),
            each(2, lambda: blocks(cap, BF16)),
            each(2, lambda: blocks(cap, BF16)),
            each(2, lambda: blocks(near * NEED + EDGES + 1, BF16)),
            each(2, pairs),
            each(2, pairs),
            each(2, lambda: blocks(near * NEED, BF16)),
            each(2, lambda: blocks(cap, BF16)),
            each(4, lambda: blocks(span, BF16)),
            blocks(EDGES, F32),
            column(EDGES + 1),
            column(EDGES + 1),
            blocks(EDGES + 1, F32),
            [column(span) for _ in range(HEADS_HERE)],
            [column(span) for _ in range(HEADS_HERE)],
            [blocks(EDGES + 1, F32) for _ in range(HEADS_HERE)],
            blocks(EDGES, BF16),
            blocks(EDGES, BF16),
            [blocks(span, F32) for _ in range(HEADS_HERE)],
            [blocks(span, F32) for _ in range(HEADS_HERE)],
            [pltpu.VMEM((span, BLOCK, 3 * BLOCK), F32) for _ in range(HEADS_HERE)],
        ]
        + [dma((HEADS_HERE, n)) for n in (4, 4, 4, 2, 2, 2, 2, 2, 2, 2, 2, 2, 2, 4, 4, 4)],
        compiler_params=pltpu.CompilerParams(
            collective_id=collective_id, has_side_effects=True, vmem_limit_bytes=56 * 2**20
        ),
        name=name,
    )
    return lax.cond(
        most_crossing(block_mask, span, groups) <= FEW,
        call(FEW, "attention_few", 0),
        call(EDGES, "attention_most", 1),
        table, query_tokens, key_tokens, value_tokens, cotangent,
    )


def solution(mesh):
    placed = P(("blk", "ulysses"), None)
    return jax.shard_map(
        shards,
        mesh=mesh,
        in_specs=(placed,) * 4 + (P(),),
        out_specs=(placed,) * 4,
        check_vma=False,
    )
```
